32 devices in a mesh: dp: 8 (over z, y), fsdp: 4 (over x, core).
Axes of the slice: x: 2, y: 2, z: 4, core: 2. Of those that a mesh axis runs over, the one named last changes fastest.
Arguments:
- queries: bfloat16 [12288, 2048], P(('dp', 'fsdp')), may hold values from -16 to 16
- passages: bfloat16 [12288, 2048], P(('dp', 'fsdp')), may hold values from -16 to 16
- weight: bfloat16 [2048, 2048], P('fsdp'), may hold values from -0.125 to 0.125
- bank: bfloat16 [256, 128, 2048], P(('dp', 'fsdp')), may hold values from -6 to 6
- neg_ids: int32 [32, 16], P(('dp', 'fsdp')), may hold values from 0 to 255, as said below
- block_home: int32 [256], replicated, may hold values from 0 to 255, as said below
Outputs:
- loss: float32 [], replicated
- grad_weight: float32 [2048, 2048], P(('dp', 'fsdp'))
- grad_queries: bfloat16 [12288, 2048], P(('dp', 'fsdp'))
- grad_passages: bfloat16 [12288, 2048], P(('dp', 'fsdp'))
The draws below stay inside these ranges and needn't reach their ends.
Inputs may be any that keep to these rules, and one draw needn't show every extreme that they name: `block_home`: A permutation of the slots; block b is held on a device whose fsdp index is b % 4. `neg_ids`: A group's 16 blocks are distinct and all held on devices of the group's own fsdp index; at most 2 of them on one device, and in every group some device holds exactly 2; in each fsdp index one device holds 2 of every group's blocks.
All inputs are finite; a program needn't handle non-finite values.
Results may differ from the reference program's by a relative error of at most 0.012.
The reference program's roundings to bfloat16 on the way (of `negs` and `grad_s`) count: a program that leaves them out, or rounds other values in their place, can miss the bound.
Values may be sent and summed in bfloat16 or wider, within the bound.
No kernel may reach another device: no remote copies, remote signals or barrier semaphores. Data moves between devices by JAX's collectives and lax.ppermute only.
A program may use at most 128 MiB of HBM per device.

```python
import math
import jax
import jax.numpy as jnp
from jax import lax

KIN = 2048
EMBED_WIDTH = 2048
QDEV = 384
BLK = 128
NEG = 16
NB_DEV = 8
QTOT = 12288
NBLK = 256
N_DP = 8
N_FSDP = 4
DEVICES = 32


def home_tables(key):
    column = N_DP * NB_DEV
    keys = jax.random.split(key, N_FSDP)
    sorted_orders = jax.vmap(lambda one: jax.random.permutation(one, column))(keys)
    lanes = jnp.arange(N_FSDP)[:, None]
    slots = (sorted_orders // NB_DEV * N_FSDP + lanes) * NB_DEV + sorted_orders % NB_DEV
    home = slots.T.reshape(NBLK).astype(jnp.int32)
    inverse = jnp.argsort(sorted_orders, axis=1, stable=True).astype(jnp.int32)
    return (home, inverse)


def draw_block_home(key, part):
    home, inverse = home_tables(key)
    return home


def draw_neg_ids(key, part):
    home, inverse = home_tables(key)
    key = jax.random.fold_in(key, 11)
    key_hot, key_perm, key_double, key_local = jax.random.split(key, 4)
    device_index = jnp.arange(DEVICES)
    lane = device_index % N_FSDP
    hot = jax.random.randint(key_hot, (N_FSDP,), 0, N_DP)[lane]
    others = jax.vmap(lambda one: jax.random.permutation(one, N_DP - 1))(jax.random.split(key_perm, DEVICES))
    rest = NEG - 2
    low = max(rest - (N_DP - 1), 0)
    doubled = jax.random.randint(key_double, (DEVICES,), low, rest // 2 + 1)
    steps = jnp.arange(rest)[None, :]
    paired = steps < 2 * doubled[:, None]
    where_at = jnp.where(paired, steps // 2, steps - doubled[:, None])
    picked = jnp.take_along_axis(others, where_at, axis=1)
    owners = jnp.concatenate([hot[:, None], hot[:, None], (hot[:, None] + 1 + picked) % N_DP], axis=1)
    copies = jnp.concatenate([jnp.zeros((DEVICES, 1), jnp.int32), jnp.ones((DEVICES, 1), jnp.int32), jnp.where(paired, steps % 2, 0).astype(jnp.int32)], axis=1)
    local_orders = jax.vmap(lambda one: jax.random.permutation(one, NB_DEV))(jax.random.split(key_local, DEVICES * N_DP))
    local_orders = local_orders.reshape(DEVICES, N_DP, NB_DEV)
    local = local_orders[device_index[:, None], owners, copies]
    column_slot = owners * NB_DEV + local
    ids = inverse[lane[:, None], column_slot] * N_FSDP + lane[:, None]
    return ids.astype(jnp.int32)


def group_ramp(low, high):
    group = (jnp.arange(QTOT) // QDEV).astype(jnp.float32)
    return (low * (high / low) ** (group / (DEVICES - 1)))[:, None]


def draw_queries(key, part):
    key = jax.random.fold_in(key, 5)
    rows = jnp.clip(jax.random.normal(key, (QTOT, KIN), jnp.float32), -6.0, 6.0)
    return (rows * group_ramp(0.5, 2.5)).astype(jnp.bfloat16)


def draw_passages(key, part):
    key = jax.random.fold_in(key, 6)
    return jnp.clip(jax.random.normal(key, (QTOT, KIN), jnp.float32), -6.0, 6.0).astype(jnp.bfloat16)


def block_levels(own_key, shape, cuts, least, largest):
    loudness = 1.0
    for dim, parts in cuts:
        heights = jax.random.uniform(jax.random.fold_in(jax.random.fold_in(own_key, 6), dim), (parts,), jnp.float32, least / len(cuts), largest / len(cuts))
        loudness = loudness * jnp.repeat(jnp.exp(heights), shape[dim] // parts).reshape((-1,) + (1,) * (len(shape) - 1 - dim))
    return loudness


def normal_values(own_key, dims, scale, reach, cuts=(), kind=jnp.bfloat16):
    level = block_levels(own_key, dims, cuts, -0.22, 0.18) if cuts else 1.0
    result = jax.random.normal(own_key, dims, jnp.float32) * scale * level
    return jnp.minimum(jnp.maximum(result, -reach), reach).astype(kind)


def setup_inputs(seed: int = 0) -> dict:
    key_of = jax.random.split(jax.random.key(seed), 7)
    return {
        "queries": draw_queries(jax.random.fold_in(key_of[6], 71), 0),
        "passages": draw_passages(jax.random.fold_in(key_of[6], 71), 0),
        "weight": normal_values(key_of[2], (KIN, EMBED_WIDTH), KIN ** -0.5, 0.125, ((0, 4),)),
        "bank": normal_values(key_of[3], (NBLK, BLK, EMBED_WIDTH), 1.0, 6.0, ((0, 32),)),
        "neg_ids": draw_neg_ids(jax.random.fold_in(key_of[6], 71), 0),
        "block_home": draw_block_home(jax.random.fold_in(key_of[6], 71), 0),
    }


SOFTMAX_TEMPER = 0.25

def reference(queries, passages, weight, bank, neg_ids, block_home):
    logit_scale = 1.0 / (SOFTMAX_TEMPER * math.sqrt(EMBED_WIDTH))
    emb_q = jnp.dot(queries, weight, preferred_element_type=jnp.float32).astype(jnp.bfloat16)
    emb_p = jnp.dot(passages, weight, preferred_element_type=jnp.float32).astype(jnp.bfloat16)
    group_q = emb_q.reshape(DEVICES, QDEV, EMBED_WIDTH)
    group_p = emb_p.reshape(DEVICES, QDEV, EMBED_WIDTH)
    slots = block_home[neg_ids].astype(jnp.int32)
    target = jnp.concatenate([jnp.eye(QDEV, dtype=jnp.float32), jnp.zeros((QDEV, NEG * BLK), jnp.float32)], axis=1)

    def group(inputs):
        q_rows, p_rows, slot_row = inputs
        negs = bank[slot_row].reshape(NEG * BLK, EMBED_WIDTH)
        inner = jnp.dot(q_rows, p_rows.T, preferred_element_type=jnp.float32) * logit_scale
        outer = jnp.dot(q_rows, negs.T, preferred_element_type=jnp.float32) * logit_scale
        scores = jnp.concatenate([inner, outer], axis=1)
        top = lax.optimization_barrier(jnp.max(scores, axis=1, keepdims=True))
        expo = jnp.exp(scores - top)
        total = lax.optimization_barrier(jnp.sum(expo, axis=1, keepdims=True))
        lse = top[:, 0] + jnp.log(total[:, 0])
        loss_sum = jnp.sum(lse - jnp.diagonal(inner))
        grad_s = ((expo / total - target) * logit_scale).astype(jnp.bfloat16)
        grad_in = grad_s[:, :QDEV]
        grad_out = grad_s[:, QDEV:]
        query_gradient = (jnp.dot(grad_in, p_rows, preferred_element_type=jnp.float32) + jnp.dot(grad_out, negs, preferred_element_type=jnp.float32)).astype(jnp.bfloat16)
        grad_p = jnp.dot(grad_in.T, q_rows, preferred_element_type=jnp.float32).astype(jnp.bfloat16)
        return (loss_sum, query_gradient, grad_p)
    losses, query_gradient, grad_p = lax.map(group, (group_q, group_p, slots))
    loss = jnp.sum(losses) / QTOT
    query_gradient = query_gradient.reshape(QTOT, EMBED_WIDTH)
    grad_p = grad_p.reshape(QTOT, EMBED_WIDTH)
    grad_weight = jnp.dot(queries.T, query_gradient, preferred_element_type=jnp.float32) + jnp.dot(passages.T, grad_p, preferred_element_type=jnp.float32)
    grad_queries = jnp.dot(query_gradient, weight.T, preferred_element_type=jnp.float32).astype(jnp.bfloat16)
    grad_passages = jnp.dot(grad_p, weight.T, preferred_element_type=jnp.float32).astype(jnp.bfloat16)
    return (loss, grad_weight, grad_queries, grad_passages)
```

```python
import functools
import math

import jax
import jax.numpy as jnp
from jax import lax
from jax.experimental import pallas as pl
from jax.experimental.pallas import tpu as pltpu
from jax.sharding import PartitionSpec as P

CAP = 2

SOFTMAX_TEMPER = 0.25

NEG_BIG = -1e30

F32 = jnp.float32
BF16 = jnp.bfloat16

VMEM_LIMIT = 32 * 1024 * 1024


def bits_of(size):
    return [1 << i for i in range(size.bit_length() - 1)]


def swap(x, axis, bit):
    return lax.ppermute(x, axis, [(i, i ^ bit) for i in range(lax.axis_size(axis))])


def dot_t(a, b):
    return lax.dot_general(a, b, (((1,), (1,)), ((), ())), preferred_element_type=F32)


def params(**kw):
    return pltpu.CompilerParams(vmem_limit_bytes=VMEM_LIMIT, **kw)


def pick_blocks(bank, ids, block_home, me, n_dp, n_fsdp):
    per_dev, block_rows, width = bank.shape
    named = ids.shape[1]
    span = per_dev * n_fsdp
    half = n_dp // 2

    def kernel(ids_ref, home_ref, me_ref, bank_ref, *refs):
        outs, table, sem = refs[:half], refs[half], refs[half + 1]
        here = me_ref[0]
        copies = []
        for k in range(half):
            for side in range(2):
                group = here ^ k ^ (side * half)
                for p in range(CAP):
                    table[p] = 0
                count = jnp.int32(0)
                for j in range(named):
                    slot = home_ref[ids_ref[group, j]]
                    mine = lax.div(slot, span) == here

                    @pl.when(mine)
                    def _():
                        table[jnp.minimum(count, CAP - 1)] = lax.rem(slot, per_dev)

                    count = count + mine.astype(jnp.int32)
                for p in range(CAP):
                    at = side * CAP + p
                    copy = pltpu.make_async_copy(
                        bank_ref.at[table[p]],
                        outs[k].at[pl.ds(at * block_rows, block_rows)],
                        sem.at[k * 2 * CAP + at],
                    )
                    copy.start()
                    copies.append(copy)
        for copy in copies:
            copy.wait()

    smem = pl.BlockSpec(memory_space=pltpu.SMEM)
    shape = (2 * CAP * block_rows, width)
    return pl.pallas_call(
        kernel,
        in_specs=[smem, smem, smem, pl.BlockSpec(memory_space=pl.ANY)],
        out_specs=[pl.BlockSpec(memory_space=pltpu.VMEM)] * half,
        out_shape=[jax.ShapeDtypeStruct(shape, bank.dtype)] * half,
        scratch_shapes=[
            pltpu.SMEM((CAP,), jnp.int32),
            pltpu.SemaphoreType.DMA((half * 2 * CAP,)),
        ],
        compiler_params=params(),
        cost_estimate=pl.CostEstimate(
            flops=0, bytes_accessed=4 * half * shape[0] * width, transcendentals=0
        ),
        name="pick_blocks",
    )(ids, block_home, me.reshape(1), bank)


def column(x):
    return jnp.max(x, axis=1, keepdims=True)


def part_scores(emb_q, emb_v, block, scale):
    count, width = emb_q.shape
    rows = block.shape[0] // 2

    def kernel(q_ref, v_ref, x_ref, own, guest):
        own[...] = dot_t(q_ref[...], x_ref[:rows]) * scale
        guest[...] = dot_t(v_ref[...], x_ref[rows:]) * scale

    return pl.pallas_call(
        kernel,
        out_shape=[jax.ShapeDtypeStruct((count, rows), F32)] * 2,
        compiler_params=params(),
        cost_estimate=pl.CostEstimate(
            flops=4 * count * rows * width,
            bytes_accessed=4 * (count + rows) * width,
            transcendentals=0,
        ),
        name="part_scores",
    )(emb_q, emb_v, block)


def pack_stats(inner, own, guest):
    count = inner.shape[0]
    n = len(own)

    def kernel(*refs):
        mine = [r[...] for r in refs[: n + 1]]
        other = [r[...] for r in refs[n + 1 : -1]]
        cols = []
        for group in (mine, other):
            top = functools.reduce(jnp.maximum, [column(s) for s in group])
            total = sum(jnp.sum(jnp.exp(s - top), axis=1, keepdims=True) for s in group)
            cols += [top, total]
        row = lax.broadcasted_iota(jnp.int32, (count, count), 0)
        col = lax.broadcasted_iota(jnp.int32, (count, count), 1)
        cols.append(jnp.sum(jnp.where(row == col, mine[0], 0.0), axis=1, keepdims=True))
        lane = lax.broadcasted_iota(jnp.int32, (count, 128), 1)
        wide = jnp.zeros((count, 128), F32)
        for i, c in enumerate(cols):
            wide = jnp.where(lane == i, c, wide)
        refs[-1][...] = wide.T[:8]

    return pl.pallas_call(
        kernel,
        out_shape=jax.ShapeDtypeStruct((8, count), F32),
        compiler_params=params(),
        name="pack_stats",
    )(inner, *own, *guest)


def joined(mine, there, a, b):
    pad = jnp.zeros((120, mine.shape[1]), F32)
    m = jnp.concatenate([mine, pad], axis=0).T
    t = jnp.concatenate([there, pad], axis=0).T
    m_top, m_sum = m[:, a : a + 1], m[:, a + 1 : a + 2]
    t_top, t_sum = t[:, b : b + 1], t[:, b + 1 : b + 2]
    top = jnp.maximum(m_top, t_top)
    return top, m_sum * jnp.exp(m_top - top) + t_sum * jnp.exp(t_top - top)


def guest_rows(scores, blocks, mine, there, scale, tile):
    count = mine.shape[1]
    n = len(scores)
    part, width = scores[0].shape[1], blocks[0].shape[1]

    def kernel(mine_ref, there_ref, *refs):
        s_refs, x_refs, out, probs = refs[:n], refs[n : 2 * n], refs[2 * n], refs[2 * n + 1]

        @pl.when(pl.program_id(0) == 0)
        def _():
            top, total = joined(mine_ref[...], there_ref[...], 2, 0)
            level = scale / total
            for k in range(n):
                probs[:, k * part : (k + 1) * part] = (
                    jnp.exp(s_refs[k][...] - top) * level
                ).astype(BF16)

        acc = jnp.zeros((count, tile), F32)
        for k in range(n):
            acc += jnp.dot(
                probs[:, k * part : (k + 1) * part], x_refs[k][...], preferred_element_type=F32
            )
        out[...] = acc.astype(BF16)

    whole = lambda a: pl.BlockSpec(a.shape, lambda i: (0, 0))
    return pl.pallas_call(
        kernel,
        grid=(width // tile,),
        in_specs=[whole(mine), whole(there)]
        + [whole(s) for s in scores]
        + [pl.BlockSpec((part, tile), lambda i: (1, i))] * n,
        out_specs=pl.BlockSpec((count, tile), lambda i: (0, i)),
        out_shape=jax.ShapeDtypeStruct((count, width), BF16),
        scratch_shapes=[pltpu.VMEM((count, n * part), BF16)],
        compiler_params=params(),
        cost_estimate=pl.CostEstimate(
            flops=2 * count * n * part * width,
            bytes_accessed=2 * n * part * width + 2 * count * width,
            transcendentals=count * n * part,
        ),
        name="guest_rows",
    )(mine, there, *scores, *blocks)


def own_rows(inner, scores, blocks, emb_q, emb_p, mine, there, scale, tile):
    count = inner.shape[0]
    n = len(scores)
    part, width = scores[0].shape[1], blocks[0].shape[1]

    def kernel(mine_ref, there_ref, inner_ref, *refs):
        s_refs, x_refs = refs[:n], refs[n : 2 * n]
        q_ref, p_ref, out, out_q, out_p, loss, probs, near, near_t = refs[2 * n :]

        @pl.when(pl.program_id(0) == 0)
        def _():
            top, total = joined(mine_ref[...], there_ref[...], 0, 2)
            level = scale / total
            for k in range(n):
                probs[:, k * part : (k + 1) * part] = (
                    jnp.exp(s_refs[k][...] - top) * level
                ).astype(BF16)
            s = inner_ref[...]
            row = lax.broadcasted_iota(jnp.int32, s.shape, 0)
            col = lax.broadcasted_iota(jnp.int32, s.shape, 1)
            target = jnp.where(row == col, 1.0, 0.0)
            grad = (jnp.exp(s - top) / total - target) * scale
            near[...] = grad.astype(BF16)
            near_t[...] = grad.T.astype(BF16)
            gtop, gtotal = joined(mine_ref[...], there_ref[...], 2, 0)
            rows = jnp.sum(top + jnp.log(total) + gtop + jnp.log(gtotal), axis=0, keepdims=True)
            lanes = jnp.sum(mine_ref[4:5, :] + there_ref[4:5, :], axis=1, keepdims=True)
            loss[...] = jnp.broadcast_to(rows - lanes, loss.shape)

        acc = jnp.dot(near[...], p_ref[...], preferred_element_type=F32)
        for k in range(n):
            acc += jnp.dot(
                probs[:, k * part : (k + 1) * part], x_refs[k][...], preferred_element_type=F32
            )
        out[...] = acc
        out_q[...] = acc.astype(BF16)
        out_p[...] = jnp.dot(near_t[...], q_ref[...], preferred_element_type=F32).astype(BF16)

    whole = lambda a: pl.BlockSpec(a.shape, lambda i: (0, 0))
    cut = lambda r: pl.BlockSpec((r, tile), lambda i: (0, i))
    return pl.pallas_call(
        kernel,
        grid=(width // tile,),
        in_specs=[whole(mine), whole(there), whole(inner)]
        + [whole(s) for s in scores]
        + [cut(part)] * n
        + [cut(count)] * 2,
        out_specs=[cut(count)] * 3 + [pl.BlockSpec((8, 128), lambda i: (0, 0))],
        out_shape=[
            jax.ShapeDtypeStruct((count, width), F32),
            jax.ShapeDtypeStruct((count, width), BF16),
            jax.ShapeDtypeStruct((count, width), BF16),
            jax.ShapeDtypeStruct((8, 128), F32),
        ],
        scratch_shapes=[
            pltpu.VMEM((count, n * part), BF16),
            pltpu.VMEM((count, count), BF16),
            pltpu.VMEM((count, count), BF16),
        ],
        compiler_params=params(),
        cost_estimate=pl.CostEstimate(
            flops=2 * count * (n * part + 2 * count) * width,
            bytes_accessed=2 * n * part * width + 12 * count * width,
            transcendentals=count * (n * part + count),
        ),
        name="own_rows",
    )(mine, there, inner, *scores, *blocks, emb_q, emb_p)


def weight_part(left, rights, base, rows_at, col_at, cols, dtype):
    quarter = left.shape[0] // 4
    count = rights[0].shape[0]
    n = len(rights)
    first, step = rows_at[0], (rows_at[1] - rows_at[0] if len(rows_at) > 1 else 1)

    def kernel(left_ref, *refs):
        acc = refs[n][...] if base is not None else jnp.zeros((quarter, cols), F32)
        for k in range(n):
            acc += jnp.dot(
                left_ref[:, k * count : (k + 1) * count],
                refs[k][...],
                preferred_element_type=F32,
            )
        refs[-1][...] = acc.astype(dtype)

    in_specs = [pl.BlockSpec((quarter, left.shape[1]), lambda i: (first + step * i, 0))]
    in_specs += [pl.BlockSpec((count, cols), lambda i: (0, col_at))] * n
    args = [left, *rights]
    if base is not None:
        in_specs.append(pl.BlockSpec((quarter, cols), lambda i: (first + step * i, col_at)))
        args.append(base)
    total = len(rows_at) * quarter
    return pl.pallas_call(
        kernel,
        grid=(len(rows_at),),
        in_specs=in_specs,
        out_specs=pl.BlockSpec((quarter, cols), lambda i: (i, 0)),
        out_shape=jax.ShapeDtypeStruct((total, cols), dtype),
        compiler_params=params(),
        cost_estimate=pl.CostEstimate(
            flops=2 * total * n * count * cols,
            bytes_accessed=2 * n * count * (cols + total) + 8 * total * cols,
            transcendentals=0,
        ),
        name="weight_part",
    )(*args)


def tied(x, after):
    return x + jnp.minimum(jnp.abs(after[:1, :1]), 0.0)


def body(queries, passages, weight, bank, neg_ids, block_home):
    count, kin = queries.shape
    width = weight.shape[1]
    scale = 1.0 / (SOFTMAX_TEMPER * math.sqrt(width))
    n_dp = lax.axis_size("dp")
    n_fsdp = lax.axis_size("fsdp")
    devices = n_dp * n_fsdp
    block_rows = bank.shape[1]
    named = neg_ids.shape[1]
    half = n_dp // 2
    me = lax.axis_index("dp")
    linear = me * n_fsdp + lax.axis_index("fsdp")

    ids = lax.all_to_all(
        jnp.broadcast_to(neg_ids, (n_dp, named)), "dp", split_axis=0, concat_axis=0, tiled=True
    )
    visit = swap(jnp.where(ids[0, 0] < 0, jnp.zeros_like(queries), queries), "dp", half)
    picked = pick_blocks(bank, ids, block_home, me, n_dp, n_fsdp)
    parts = [picked[0]] + [swap(picked[k], "dp", k) for k in range(1, half)]

    full_weight = lax.all_gather(weight, "fsdp", axis=0, tiled=True)
    emb_q = jnp.dot(queries, full_weight, preferred_element_type=F32).astype(BF16)
    emb_p = jnp.dot(passages, full_weight, preferred_element_type=F32).astype(BF16)
    emb_v = jnp.dot(visit, full_weight, preferred_element_type=F32).astype(BF16)

    f_bits = [("fsdp", b) for b in bits_of(n_fsdp)]
    d_bits = [("dp", b) for b in bits_of(n_dp)]
    stages = [f_bits[1], d_bits[0]] + f_bits[2:] + d_bits[1:]
    mask = []
    for p in range(devices // 2):
        m = 0
        for s, (axis, bit) in enumerate(stages):
            if not (p >> (len(stages) - 1 - s)) & 1:
                m |= bit if axis == "fsdp" else bit * n_fsdp
        mask.append(m)
    mask = jnp.array(mask, jnp.int32)
    hidden_t = jnp.concatenate([queries, passages, visit], axis=0).T
    hidden_t = hidden_t.reshape(devices, kin // devices, -1)
    left = jnp.take(hidden_t, linear ^ mask, axis=0).reshape(kin // 2, -1)
    left_out = jnp.take(hidden_t, linear ^ 1 ^ mask, axis=0).reshape(kin // 2, -1)
    left_in = swap(left_out, *f_bits[0])

    masked = n_dp * CAP > named
    if masked:
        owner = block_home[ids] // bank.shape[0] // n_fsdp

    inner = dot_t(emb_q, emb_p) * scale
    s_own, s_guest = [], []
    for k, x in enumerate(parts):
        pair = list(part_scores(emb_q, emb_v, x, scale))
        if masked:
            for i, group in enumerate((me, me ^ half)):
                held = jnp.sum((owner[group] == (me ^ k)).astype(jnp.int32))
                there = jnp.arange(CAP * block_rows) // block_rows < held
                pair[i] = jnp.where(there[None, :], pair[i], NEG_BIG)
        s_own.append(pair[0])
        s_guest.append(pair[1])

    mine = pack_stats(inner, s_own, s_guest)
    there = swap(mine, "dp", half)
    tile = 512
    rows_v = guest_rows(s_guest, parts, mine, there, scale, tile)
    home = swap(rows_v, "dp", half)
    rows_own, rows_q, rows_p, loss = own_rows(
        inner, s_own, parts, emb_q, emb_p, mine, there, scale, tile
    )

    rights = [rows_q, rows_p, rows_v]
    far_rights = [swap(r, *f_bits[0]) for r in rights]
    base = weight_part(left, rights, None, (0, 1, 2, 3), 0, width, F32)
    cols = width // 2
    give = ((0, 1), (0, 2))
    hold = ((2, 3), (1, 3))
    sends = [weight_part(left_in, far_rights, base, give[i], i, cols, BF16) for i in range(2)]
    keeps = [weight_part(left_in, far_rights, base, hold[i], i, cols, F32) for i in range(2)]
    orders = [stages, [stages[1], stages[0]] + stages[2:]]

    loss = loss[:1, :1]
    for axis, bit in f_bits + d_bits[:-2]:
        loss = loss + swap(loss, axis, bit)

    mid = kin // 4
    for s in range(len(stages)):
        last = s + 1 == len(stages)
        if last:
            loss = tied(loss, keeps[0])
            loss = loss + swap(loss, *d_bits[-2])
        got = [swap(sends[i], *orders[i][s]) for i in range(2)]
        keeps = [keeps[i] + got[i].astype(F32) for i in range(2)]
        if not last:
            mid = mid // 2
            sends = [k[:mid].astype(BF16) for k in keeps]
            keeps = [k[mid:] for k in keeps]
    grad_weight = jnp.concatenate(keeps, axis=1)
    loss = loss[0, 0] / (count * devices)

    back_p = dot_t(rows_p, full_weight).astype(BF16)
    both = (rows_own + home.astype(F32)).astype(BF16)
    back_q = dot_t(both, full_weight).astype(BF16)
    return (loss, grad_weight, back_q, back_p)


def solution(mesh):
    return jax.shard_map(
        body,
        mesh=mesh,
        in_specs=(
            P(("dp", "fsdp"), None),
            P(("dp", "fsdp"), None),
            P("fsdp", None),
            P(("dp", "fsdp"), None, None),
            P(("dp", "fsdp"), None),
            P(),
        ),
        out_specs=(P(), P(("dp", "fsdp"), None), P(("dp", "fsdp"), None), P(("dp", "fsdp"), None)),
        check_vma=False,
    )
```

```python
import functools
import math

import jax
import jax.numpy as jnp
from jax import lax
from jax.experimental import pallas as pl
from jax.experimental.pallas import tpu as pltpu
from jax.sharding import PartitionSpec as P

CAP = 2

SOFTMAX_TEMPER = 0.25

NEG_BIG = -1e30

TAIL = 16

F32 = jnp.float32
BF16 = jnp.bfloat16

VMEM_LIMIT = 24 * 1024 * 1024


def bits_of(size):
    return [1 << i for i in range(size.bit_length() - 1)]


def swap(x, axis, bit):
    return lax.ppermute(x, axis, [(i, i ^ bit) for i in range(lax.axis_size(axis))])


def move(x, bit_of):
    n_dp, n_fsdp = lax.axis_size("dp"), lax.axis_size("fsdp")
    pairs = [
        (i * n_fsdp + f, (i ^ bit_of(f)) * n_fsdp + f) for i in range(n_dp) for f in range(n_fsdp)
    ]
    return lax.ppermute(x, ("dp", "fsdp"), pairs)


def dot_t(a, b):
    return lax.dot_general(a, b, (((1,), (1,)), ((), ())), preferred_element_type=F32)


ANY = pl.BlockSpec(memory_space=pl.ANY)


def params(**kw):
    return pltpu.CompilerParams(vmem_limit_bytes=VMEM_LIMIT, **kw)


def pick_blocks(bank, ids, block_home, me, n_dp, n_fsdp):
    per_dev, block_rows, width = bank.shape
    named = ids.shape[1]
    span = per_dev * n_fsdp
    half = n_dp // 2
    rows = CAP * block_rows

    def kernel(ids_ref, home_ref, me_ref, bank_ref, own, *refs):
        guests, none, table, held, sem, whole_sem = refs[:half], *refs[half:]
        load = pltpu.make_async_copy(bank_ref, held, whole_sem)
        load.start()
        here = me_ref[0]
        none[...] = jnp.zeros(none.shape, none.dtype)
        base = here & half
        targets = [(here ^ k ^ half, guests[k], 0) for k in range(half)]
        targets += [(base + k, own, k * rows) for k in range(half)]
        for t, (group, _, _) in enumerate(targets):
            for p in range(CAP):
                table[t * CAP + p] = 0
            count = jnp.int32(0)
            for j in range(named):
                slot = home_ref[ids_ref[group, j]]
                mine = lax.div(slot, span) == here

                @pl.when(mine)
                def _():
                    table[t * CAP + jnp.minimum(count, CAP - 1)] = lax.rem(slot, per_dev)

                count = count + mine.astype(jnp.int32)
        load.wait()
        copies = []
        for t, (_, out, at) in enumerate(targets):
            for p in range(CAP):
                copy = pltpu.make_async_copy(
                    held.at[table[t * CAP + p]],
                    out.at[pl.ds(at + p * block_rows, block_rows)],
                    sem.at[len(copies)],
                )
                copy.start()
                copies.append(copy)
        for copy in copies:
            copy.wait()

    smem = pl.BlockSpec(memory_space=pltpu.SMEM)
    return pl.pallas_call(
        kernel,
        in_specs=[smem, smem, smem, ANY],
        out_specs=[ANY] * (half + 1) + [pl.BlockSpec(memory_space=pltpu.VMEM)],
        out_shape=[jax.ShapeDtypeStruct((half * rows, width), bank.dtype)]
        + [jax.ShapeDtypeStruct((rows, width), bank.dtype)] * half
        + [jax.ShapeDtypeStruct((8, 128), jnp.int32)],
        scratch_shapes=[
            pltpu.SMEM((n_dp * CAP,), jnp.int32),
            pltpu.VMEM(bank.shape, bank.dtype),
            pltpu.SemaphoreType.DMA((n_dp * CAP,)),
            pltpu.SemaphoreType.DMA,
        ],
        compiler_params=params(),
        cost_estimate=pl.CostEstimate(
            flops=0, bytes_accessed=4 * n_dp * rows * width, transcendentals=0
        ),
        name="pick_blocks",
    )(ids, block_home, me.reshape(1), bank)


def part_scores(emb, x, rows, held, scale, emb_p=None, before=None, pack=False, after=()):
    count, width = emb.shape
    sets = x.shape[0] // rows

    def kernel(*refs):
        refs = list(refs)
        held_ref = refs.pop(0) if held is not None else None
        emb_ref, x_ref = refs.pop(0), refs.pop(0)
        p_ref = refs.pop(0) if emb_p is not None else None
        before_ref = refs.pop(0) if before is not None else None
        del refs[: len(after)]
        out, stats, state = refs[0], refs[1], refs[-1]
        step = pl.program_id(0)

        def fold(s):
            groups = [s[:, i : i + 128] for i in range(0, s.shape[1], 128)]
            old = state[:, :128]
            top = functools.reduce(jnp.maximum, groups, old)
            total = state[:, 128:] * jnp.exp(old - top)
            state[:, :128] = top
            state[:, 128:] = total + sum(jnp.exp(g - top) for g in groups)

        @pl.when(step == 0)
        def _():
            if before is not None:
                state[...] = before_ref[...]
            else:
                state[:, :128] = jnp.full((count, 128), NEG_BIG, F32)
                state[:, 128:] = jnp.zeros((count, 128), F32)
            if emb_p is not None:
                inner = dot_t(emb_ref[...], p_ref[...]) * scale
                refs[2][...] = inner
                fold(inner)

        s = dot_t(emb_ref[...], x_ref[...]) * scale
        if held is not None:
            col = lax.broadcasted_iota(jnp.int32, s.shape, 1)
            s = jnp.where(col < held_ref[step], s, NEG_BIG)
        out[...] = s
        fold(s)

        @pl.when(step == sets - 1)
        def _():
            if pack:
                tops = state[:, :128].T
                top = jnp.max(tops, axis=0, keepdims=True)
                total = jnp.sum(state[:, 128:].T * jnp.exp(tops - top), axis=0, keepdims=True)
                row = lax.broadcasted_iota(jnp.int32, (8, count), 0)
                stats[...] = jnp.where(row == 0, top, total)
            else:
                stats[...] = state[...]

    whole = lambda a: pl.BlockSpec(a.shape, lambda i: (0, 0))
    args, in_specs = [emb, x], [whole(emb), pl.BlockSpec((rows, width), lambda i: (i, 0))]
    for a in (emb_p, before):
        if a is not None:
            args.append(a)
            in_specs.append(whole(a))
    args += after
    in_specs += [ANY] * len(after)
    if held is not None:
        args.insert(0, held)
        in_specs.insert(0, pl.BlockSpec(memory_space=pltpu.SMEM))
    stats_shape = (8, count) if pack else (count, 256)
    out_shape = [
        jax.ShapeDtypeStruct((count, x.shape[0]), F32),
        jax.ShapeDtypeStruct(stats_shape, F32),
    ]
    out_specs = [
        pl.BlockSpec((count, rows), lambda i: (0, i)),
        pl.BlockSpec(stats_shape, lambda i: (0, 0)),
    ]
    if emb_p is not None:
        out_shape.append(jax.ShapeDtypeStruct((count, count), F32))
        out_specs.append(pl.BlockSpec((count, count), lambda i: (0, 0)))
    return pl.pallas_call(
        kernel,
        grid=(sets,),
        in_specs=in_specs,
        out_specs=out_specs,
        out_shape=out_shape,
        scratch_shapes=[pltpu.VMEM((count, 256), F32)],
        compiler_params=params(),
        cost_estimate=pl.CostEstimate(
            flops=2 * count * x.shape[0] * width,
            bytes_accessed=2 * (count + x.shape[0]) * width,
            transcendentals=2 * count * x.shape[0],
        ),
        name="part_scores",
    )(*args)


def joined(mine, there):
    pad = jnp.zeros((120, mine.shape[1]), F32)
    m = jnp.concatenate([mine, pad], axis=0).T
    t = jnp.concatenate([there, pad], axis=0).T
    top = jnp.maximum(m[:, 0:1], t[:, 0:1])
    return top, m[:, 1:2] * jnp.exp(m[:, 0:1] - top) + t[:, 1:2] * jnp.exp(t[:, 0:1] - top)


def split_rows(x, cols):
    hi = x.astype(BF16).astype(F32)
    mid = (x - hi).astype(BF16).astype(F32)
    low = (x - hi - mid).astype(BF16).astype(F32)
    row = lax.broadcasted_iota(jnp.int32, (TAIL, cols), 0)
    wide = jnp.where(row == 0, hi, jnp.where(row == 1, mid, jnp.where(row == 2, low, 0.0)))
    return wide.astype(BF16)


def joined_rows(x):
    return jnp.sum(x[:, :128].astype(F32), axis=0, keepdims=True)[:, :1]


def guest_rows(mine, there, scores, guests, stays, scale, tile, after):
    count = mine.shape[1]
    n = len(guests)
    part, width = guests[0].shape
    tiles = width // tile

    def kernel(stays_ref, mine_ref, there_ref, *refs):
        s_refs, x_refs = refs[:n], refs[n : 2 * n]
        full, backs, probs = refs[2 * n + 1], refs[2 * n + 2 : -1], refs[-1]

        @pl.when(pl.program_id(0) == 0)
        def _():
            top, total = joined(mine_ref[...], there_ref[...])
            level = scale / total
            for k in range(n):
                probs[:, k * part : (k + 1) * part] = (
                    jnp.exp(s_refs[k][...] - top) * level
                ).astype(BF16)

        far = jnp.zeros((count, tile), F32)
        for k in range(n):
            far += jnp.dot(
                probs[:, k * part : (k + 1) * part], x_refs[k][...], preferred_element_type=F32
            )
        full[...] = far
        far = jnp.where(stays_ref[0] > 0, 0.0, far).astype(BF16)
        for i in range(tiles):

            @pl.when(pl.program_id(0) == i)
            def _():
                backs[i][...] = far

    whole = lambda a: pl.BlockSpec(a.shape, lambda i: (0, 0))
    return pl.pallas_call(
        kernel,
        grid=(tiles,),
        in_specs=[pl.BlockSpec(memory_space=pltpu.SMEM), whole(mine), whole(there)]
        + [whole(s) for s in scores]
        + [pl.BlockSpec((part, tile), lambda i: (0, i))] * n
        + [ANY],
        out_specs=[pl.BlockSpec((count, tile), lambda i: (0, i))]
        + [pl.BlockSpec((count, tile), lambda i: (0, 0))] * tiles,
        out_shape=[jax.ShapeDtypeStruct((count, width), F32)]
        + [jax.ShapeDtypeStruct((count, tile), BF16)] * tiles,
        scratch_shapes=[pltpu.VMEM((count, n * part), BF16)],
        compiler_params=params(),
        cost_estimate=pl.CostEstimate(
            flops=2 * count * n * part * width,
            bytes_accessed=2 * n * part * width + 6 * count * width,
            transcendentals=count * n * part,
        ),
        name="guest_rows",
    )(stays, mine, there, *scores, *guests, after)


def own_grads(mine, there, inner, own, scale):
    count = inner.shape[0]

    def kernel(mine_ref, there_ref, inner_ref, own_ref, out, near, near_t, loss):
        top, total = joined(mine_ref[...], there_ref[...])
        out[...] = (jnp.exp(own_ref[...] - top) * (scale / total)).astype(BF16)
        s = inner_ref[...]
        row = lax.broadcasted_iota(jnp.int32, s.shape, 0)
        col = lax.broadcasted_iota(jnp.int32, s.shape, 1)
        target = jnp.where(row == col, 1.0, 0.0)
        grad = (jnp.exp(s - top) / total - target) * scale
        near[...] = grad.astype(BF16)
        near_t[...] = grad.T.astype(BF16)
        rows = top + jnp.log(total) - jnp.sum(s * target, axis=1, keepdims=True)
        loss[...] = jnp.broadcast_to(jnp.sum(rows, axis=0, keepdims=True), loss.shape)

    wide = jax.ShapeDtypeStruct(own.shape, BF16)
    square = jax.ShapeDtypeStruct((count, count), BF16)
    return pl.pallas_call(
        kernel,
        out_shape=[wide, square, square, jax.ShapeDtypeStruct((8, 128), F32)],
        compiler_params=params(),
        cost_estimate=pl.CostEstimate(
            flops=8 * count * (own.shape[1] + count),
            bytes_accessed=6 * count * (own.shape[1] + count),
            transcendentals=count * (own.shape[1] + count),
        ),
        name="own_grads",
    )(mine, there, inner, own)


def grad_rows(p_own, near, near_t, own, emb_q, emb_p, far, backs, loss, stays, tile, start, before):
    count = near.shape[0]
    tiles = len(backs)
    total, width = own.shape

    def kernel(stays_ref, own_ref, near_ref, near_t_ref, x_ref, q_ref, p_ref, far_ref, *refs):
        back_refs, loss_ref = refs[:tiles], refs[tiles]
        outs, full = refs[-tiles - 1 : -1], refs[-1]
        acc = jnp.dot(near_ref[...], p_ref[...], preferred_element_type=F32)
        acc += jnp.dot(own_ref[...], x_ref[...], preferred_element_type=F32)
        acc += jnp.where(stays_ref[0] > 0, far_ref[...], 0.0)
        full[...] = acc
        pos = jnp.dot(near_t_ref[...], q_ref[...], preferred_element_type=F32).astype(BF16)
        acc = acc.astype(BF16)
        tail = split_rows(loss_ref[0:1, 0:1], tile)
        for i in range(tiles):

            @pl.when(pl.program_id(0) == i)
            def _():
                outs[i][:count] = acc
                outs[i][count : 2 * count] = pos
                outs[i][2 * count : 3 * count] = back_refs[i][...]
                outs[i][3 * count :] = tail

    whole = lambda a: pl.BlockSpec(a.shape, lambda i: (0, 0))
    cut = lambda r: pl.BlockSpec((r, tile), lambda i: (0, start + i))
    args = [stays, p_own, near, near_t, own, emb_q, emb_p, far, *backs, loss, *before]
    return pl.pallas_call(
        kernel,
        grid=(tiles,),
        in_specs=[pl.BlockSpec(memory_space=pltpu.SMEM)]
        + [whole(p_own), whole(near), whole(near_t), cut(total)]
        + [cut(count)] * 3
        + [whole(b) for b in backs]
        + [whole(loss)]
        + [ANY] * len(before),
        out_specs=[pl.BlockSpec((3 * count + TAIL, tile), lambda i: (0, 0))] * tiles
        + [cut(count)],
        out_shape=[jax.ShapeDtypeStruct((3 * count + TAIL, tile), BF16)] * tiles
        + [jax.ShapeDtypeStruct((count, width), F32)],
        input_output_aliases={len(args) - len(before) + i: tiles + i for i in range(len(before))},
        compiler_params=params(),
        cost_estimate=pl.CostEstimate(
            flops=2 * count * (total + 2 * count) * tile * tiles,
            bytes_accessed=(2 * total + 20 * count) * tile * tiles,
            transcendentals=0,
        ),
        name="grad_rows",
    )(*args)


def last_product(pieces, at, count, weight, tile, full=None, after=()):
    kin, width = weight.shape
    n = len(pieces)
    cols = pieces[0].shape[1]

    def kernel(w_ref, *refs):
        out, rows = refs[-2], refs[-1]

        @pl.when(pl.program_id(0) == 0)
        def _():
            for k in range(n):
                piece = refs[k][...]
                if full is not None:
                    piece = refs[n][:, k * cols : (k + 1) * cols] + piece.astype(F32)
                rows[:, k * cols : (k + 1) * cols] = piece.astype(BF16)

        out[...] = dot_t(rows[...], w_ref[...]).astype(BF16)

    args = [weight, *pieces]
    in_specs = [pl.BlockSpec((tile, width), lambda i: (i, 0))]
    in_specs += [pl.BlockSpec((count, cols), lambda i: (at, 0))] * n
    if full is not None:
        args.append(full)
        in_specs.append(pl.BlockSpec((count, width), lambda i: (0, 0)))
    return pl.pallas_call(
        kernel,
        grid=(kin // tile,),
        in_specs=in_specs + [ANY] * len(after),
        out_specs=pl.BlockSpec((count, tile), lambda i: (0, i)),
        out_shape=jax.ShapeDtypeStruct((count, kin), BF16),
        scratch_shapes=[pltpu.VMEM((count, width), BF16)],
        compiler_params=params(),
        cost_estimate=pl.CostEstimate(
            flops=2 * count * width * kin,
            bytes_accessed=2 * width * kin + 4 * count * (width + kin),
            transcendentals=0,
        ),
        name="last_product",
    )(*args, *after)


def weight_part(left, at, rights, base, rows_at, dtype, tails=(), after=()):
    depth, tile = left.shape[1], rights[0].shape[1]
    n, m = len(rights), len(rows_at)
    quarter = left.shape[0] // (8 if at is not None else 4)
    at = at or 0
    first, step = rows_at[0], rows_at[1] - rows_at[0]
    total = m * quarter

    def kernel(left_ref, *refs):
        out = refs[-2] if tails else refs[-1]
        if tails:
            rows = pl.ds(pl.multiple_of(pl.program_id(0) * quarter, quarter), quarter)
        else:
            rows = slice(None)
        for k in range(n):
            cols = slice(k * tile, (k + 1) * tile)
            acc = jnp.dot(left_ref[...], refs[k][...], preferred_element_type=F32)
            if base is not None:
                acc += refs[n][:, cols]
            out[rows, cols] = acc.astype(dtype)
        if tails:
            loss = sum(joined_rows(r[...]) for r in refs[n + 1 : n + 1 + len(tails)])
            out[total:, :] = split_rows(loss, n * tile)
            refs[-1][...] = jnp.broadcast_to(loss, refs[-1].shape)

    in_specs = [pl.BlockSpec((quarter, depth), lambda i: (at + first + step * i, 0))]
    in_specs += [pl.BlockSpec((depth, tile), lambda i: (0, 0))] * n
    args = [left, *rights]
    if base is not None:
        in_specs.append(pl.BlockSpec((quarter, n * tile), lambda i: (first + step * i, 0)))
        args.append(base)
    for t in tails:
        in_specs.append(pl.BlockSpec((TAIL, tile), lambda i: (depth // TAIL, 0)))
        args.append(t)
    in_specs += [ANY] * len(after)
    args += after
    if tails:
        shape = (total + TAIL, n * tile)
        out_shape = [jax.ShapeDtypeStruct(shape, dtype), jax.ShapeDtypeStruct((8, 128), F32)]
        out_specs = [pl.BlockSpec(s.shape, lambda i: (0, 0)) for s in out_shape]
    else:
        out_shape = jax.ShapeDtypeStruct((total, n * tile), dtype)
        out_specs = pl.BlockSpec((quarter, n * tile), lambda i: (i, 0))
    return pl.pallas_call(
        kernel,
        grid=(m,),
        in_specs=in_specs,
        out_specs=out_specs,
        out_shape=out_shape,
        compiler_params=params(),
        cost_estimate=pl.CostEstimate(
            flops=2 * total * n * depth * tile,
            bytes_accessed=2 * depth * (n * tile + total) + 8 * total * n * tile,
            transcendentals=0,
        ),
        name="weight_part",
    )(*args)


def fold_stage(keep, got, loss=None, after=()):
    rows, cols = keep.shape
    mid = rows // 2

    def kernel(keep_ref, got_ref, *refs):
        if loss is None:
            send, rest = refs[-2:]
        else:
            send, rest, state = refs[-3:]
            value = refs[0][0:1, 0:1] + joined_rows(got_ref[rows:])
            state[...] = jnp.broadcast_to(value, state.shape)
            send[mid:] = split_rows(value, cols)
        send[:mid] = (keep_ref[:mid] + got_ref[:mid].astype(F32)).astype(BF16)
        rest[...] = keep_ref[mid:] + got_ref[mid:rows].astype(F32)

    args = [keep, got] + ([loss] if loss is not None else [])
    in_specs = [pl.BlockSpec(memory_space=pltpu.VMEM)] * len(args)
    args += after
    in_specs += [ANY] * len(after)
    out_shape = [
        jax.ShapeDtypeStruct((mid + (TAIL if loss is not None else 0), cols), BF16),
        jax.ShapeDtypeStruct((rows - mid, cols), F32),
    ]
    if loss is not None:
        out_shape.append(jax.ShapeDtypeStruct((8, 128), F32))
    return pl.pallas_call(
        kernel,
        in_specs=in_specs,
        out_shape=out_shape,
        compiler_params=params(),
        cost_estimate=pl.CostEstimate(
            flops=rows * cols, bytes_accessed=9 * rows * cols, transcendentals=0
        ),
        name="fold_stage",
    )(*args)


def last_stage(keeps, gots, loss):
    rows, cols = keeps[0].shape

    def kernel(keep0, got0, keep1, got1, loss_ref, out, state):
        out[:, :cols] = keep0[...] + got0[:rows].astype(F32)
        out[:, cols:] = keep1[...] + got1[:rows].astype(F32)
        state[...] = loss_ref[...] + joined_rows(got0[rows:])

    return pl.pallas_call(
        kernel,
        out_shape=[
            jax.ShapeDtypeStruct((rows, 2 * cols), F32),
            jax.ShapeDtypeStruct((8, 128), F32),
        ],
        compiler_params=params(),
        name="last_stage",
    )(keeps[0], gots[0], keeps[1], gots[1], loss)


def body(queries, passages, weight, bank, neg_ids, block_home):
    count, kin = queries.shape
    width = weight.shape[1]
    scale = 1.0 / (SOFTMAX_TEMPER * math.sqrt(width))
    n_dp = lax.axis_size("dp")
    n_fsdp = lax.axis_size("fsdp")
    devices = n_dp * n_fsdp
    block_rows = bank.shape[1]
    named = neg_ids.shape[1]
    half = n_dp // 2
    me = lax.axis_index("dp")
    core = lax.axis_index("fsdp") % 2
    linear = me * n_fsdp + lax.axis_index("fsdp")

    trip = lambda f: half if f % 2 == 0 else 0

    ids = lax.all_to_all(
        jnp.broadcast_to(neg_ids, (n_dp, named)), "dp", split_axis=0, concat_axis=0, tiled=True
    )
    leaving = jnp.where(ids[0, 0] < 0, jnp.zeros_like(queries), queries)
    visit = move(leaving, trip)
    own, *guests, zero = pick_blocks(bank, ids, block_home, me, n_dp, n_fsdp)
    guests = [
        move(g, lambda f, k=k: k if f % 2 == 0 else k ^ half) for k, g in enumerate(guests)
    ]
    sides = [list(range(half)), list(range(half, n_dp))]
    own = lax.all_to_all(
        own, "dp", split_axis=0, concat_axis=0, tiled=True, axis_index_groups=sides
    )
    late = jnp.where(zero[0, 0] < 0, jnp.zeros_like(passages), passages)

    full_weight = lax.all_gather(weight, "fsdp", axis=0, tiled=True)
    emb_q = jnp.dot(queries, full_weight, preferred_element_type=F32).astype(BF16)
    emb_p = jnp.dot(passages, full_weight, preferred_element_type=F32).astype(BF16)
    emb_v = jnp.dot(visit, full_weight, preferred_element_type=F32).astype(BF16)

    f_bits = [("fsdp", b) for b in bits_of(n_fsdp)]
    d_bits = [("dp", b) for b in bits_of(n_dp)]
    stages = [f_bits[1], d_bits[0]] + f_bits[2:] + d_bits[1:]
    mask = []
    for p in range(devices // 2):
        m = 0
        for s, (axis, bit) in enumerate(stages):
            if not (p >> (len(stages) - 1 - s)) & 1:
                m |= bit if axis == "fsdp" else bit * n_fsdp
        mask.append(m)
    mask = jnp.array(mask, jnp.int32)
    hidden_t = jnp.concatenate([queries, late, visit], axis=0).T
    hidden_t = hidden_t.reshape(devices, kin // devices, -1)
    order = linear ^ jnp.concatenate([mask ^ 1, mask])
    left = jnp.take(hidden_t, order, axis=0).reshape(kin, -1)
    left_in = swap(left[: kin // 2], *f_bits[0])

    masked = n_dp * CAP > named
    own_held, guest_held = None, [None] * half
    if masked:
        owner = block_home[ids] // bank.shape[0] // n_fsdp
        held = lambda g, by: (jnp.sum(owner[g] == by) * block_rows).astype(jnp.int32)
        far = jnp.where(core == 0, 0, half)
        own_held = jnp.stack([held(me, (me & half) + k) for k in range(half)])
        guest_held = [held(me ^ half ^ far, me ^ k ^ far).reshape(1) for k in range(half)]
    rows = CAP * block_rows
    s_own, own_stats, inner = part_scores(
        emb_q, own, rows, own_held, scale, emb_p=emb_p, pack=True
    )
    their_stats = move(own_stats, trip)
    s_guest, stats = [], None
    for k, x in enumerate(guests):
        after = (inner,) if k == half // 2 else ()
        s, stats = part_scores(
            emb_v, x, rows, guest_held[k], scale, before=stats, pack=k == half - 1, after=after
        )
        s_guest.append(s)

    far_stats = move(stats, trip)
    tile = width // 4
    stays = core.astype(jnp.int32).reshape(1)
    far, *backs = guest_rows(
        stats, their_stats, s_guest, guests, stays, scale, tile, left_in
    )
    home = [move(r, trip) for r in backs]
    p_own, near, near_t, loss = own_grads(own_stats, far_stats, inner, s_own, scale)
    rows, kept = [], ()
    for i in range(2):
        *g, full = grad_rows(
            p_own,
            near,
            near_t,
            own,
            emb_q,
            emb_p,
            far,
            backs[2 * i : 2 * i + 2],
            loss,
            stays,
            tile,
            2 * i,
            kept,
        )
        rows += g
        kept = (full,)
    far_rows = [swap(r, *f_bits[0]) for r in rows]

    orders = [stages, [stages[1], stages[0]] + stages[2:]]
    give = ((0, 1), (0, 2))
    hold = ((2, 3), (1, 3))
    every = (0, 1, 2, 3)
    bases = [
        weight_part(left, 4, rows[:2], None, every, F32),
        weight_part(left, 4, rows[2:], None, every, F32, after=(home[0],)),
    ]
    got = [far_rows[:2], far_rows[2:]]
    send, loss = weight_part(
        left_in, None, got[0], bases[0], give[0], BF16, tails=(rows[0], far_rows[0])
    )
    sends = [send, weight_part(left_in, None, got[1], bases[1], give[1], BF16, after=(home[1],))]
    back_p = last_product(rows, 1, count, full_weight, tile, after=(sends[1],))
    keeps = [
        weight_part(left_in, None, got[0], bases[0], hold[0], F32),
        weight_part(left_in, None, got[1], bases[1], hold[1], F32),
    ]
    waits = {(0, 0): (back_p, keeps[1]), (0, 1): (home[2], home[3])}
    for s in range(len(stages)):
        gots = [swap(sends[i], *orders[i][s]) for i in range(2)]
        if s + 1 < len(stages):
            send0, keep0, loss = fold_stage(keeps[0], gots[0], loss, waits.get((s, 0), ()))
            send1, keep1 = fold_stage(keeps[1], gots[1], after=waits.get((s, 1), ()))
            sends, keeps = [send0, send1], [keep0, keep1]
    back_q = last_product(home, 0, count, full_weight, tile, full=full, after=tuple(sends))
    grad_weight, loss = last_stage(keeps, gots, loss)
    loss = loss[0, 0] / (count * devices)
    return (loss, grad_weight, back_q, back_p)


def solution(mesh):
    return jax.shard_map(
        body,
        mesh=mesh,
        in_specs=(
            P(("dp", "fsdp"), None),
            P(("dp", "fsdp"), None),
            P("fsdp", None),
            P(("dp", "fsdp"), None, None),
            P(("dp", "fsdp"), None),
            P(),
        ),
        out_specs=(P(), P(("dp", "fsdp"), None), P(("dp", "fsdp"), None), P(("dp", "fsdp"), None)),
        check_vma=False,
    )
```

```python
import functools
import math

import jax
import jax.numpy as jnp
from jax import lax
from jax.experimental import pallas as pl
from jax.experimental.pallas import tpu as pltpu
from jax.sharding import PartitionSpec as P

CAP = 2

SOFTMAX_TEMPER = 0.25

NEG_BIG = -1e30

TAIL = 16

F32 = jnp.float32
BF16 = jnp.bfloat16

VMEM_LIMIT = 24 * 1024 * 1024


def bits_of(size):
    return [1 << i for i in range(size.bit_length() - 1)]


def swap(x, axis, bit):
    return lax.ppermute(x, axis, [(i, i ^ bit) for i in range(lax.axis_size(axis))])


def move(x, bit_of):
    n_dp, n_fsdp = lax.axis_size("dp"), lax.axis_size("fsdp")
    pairs = [
        (i * n_fsdp + f, (i ^ bit_of(f)) * n_fsdp + f) for i in range(n_dp) for f in range(n_fsdp)
    ]
    return lax.ppermute(x, ("dp", "fsdp"), pairs)


def dot_t(a, b):
    return lax.dot_general(a, b, (((1,), (1,)), ((), ())), preferred_element_type=F32)


ANY = pl.BlockSpec(memory_space=pl.ANY)


def params(**kw):
    return pltpu.CompilerParams(vmem_limit_bytes=VMEM_LIMIT, **kw)


def pick_blocks(bank, ids, block_home, me, n_dp, n_fsdp):
    per_dev, block_rows, width = bank.shape
    named = ids.shape[1]
    span = per_dev * n_fsdp
    half = n_dp // 2
    rows = CAP * block_rows

    def kernel(ids_ref, home_ref, me_ref, bank_ref, own, *refs):
        guests, none, table, held, sem, whole_sem = refs[:half], *refs[half:]
        load = pltpu.make_async_copy(bank_ref, held, whole_sem)
        load.start()
        here = me_ref[0]
        none[...] = jnp.zeros(none.shape, none.dtype)
        base = here & half
        targets = [(here ^ k ^ half, guests[k], 0) for k in range(half)]
        targets += [(base + k, own, k * rows) for k in range(half)]
        for t, (group, _, _) in enumerate(targets):
            for p in range(CAP):
                table[t * CAP + p] = 0
            count = jnp.int32(0)
            for j in range(named):
                slot = home_ref[ids_ref[group, j]]
                mine = lax.div(slot, span) == here

                @pl.when(mine)
                def _():
                    table[t * CAP + jnp.minimum(count, CAP - 1)] = lax.rem(slot, per_dev)

                count = count + mine.astype(jnp.int32)
        load.wait()
        copies = []
        for t, (_, out, at) in enumerate(targets):
            for p in range(CAP):
                copy = pltpu.make_async_copy(
                    held.at[table[t * CAP + p]],
                    out.at[pl.ds(at + p * block_rows, block_rows)],
                    sem.at[len(copies)],
                )
                copy.start()
                copies.append(copy)
        for copy in copies:
            copy.wait()

    smem = pl.BlockSpec(memory_space=pltpu.SMEM)
    return pl.pallas_call(
        kernel,
        in_specs=[smem, smem, smem, ANY],
        out_specs=[ANY] * (half + 1) + [pl.BlockSpec(memory_space=pltpu.VMEM)],
        out_shape=[jax.ShapeDtypeStruct((half * rows, width), bank.dtype)]
        + [jax.ShapeDtypeStruct((rows, width), bank.dtype)] * half
        + [jax.ShapeDtypeStruct((8, 128), jnp.int32)],
        scratch_shapes=[
            pltpu.SMEM((n_dp * CAP,), jnp.int32),
            pltpu.VMEM(bank.shape, bank.dtype),
            pltpu.SemaphoreType.DMA((n_dp * CAP,)),
            pltpu.SemaphoreType.DMA,
        ],
        compiler_params=params(),
        cost_estimate=pl.CostEstimate(
            flops=0, bytes_accessed=4 * n_dp * rows * width, transcendentals=0
        ),
        name="pick_blocks",
    )(ids, block_home, me.reshape(1), bank)


def part_scores(emb, x, rows, held, scale, emb_p=None, before=None, pack=False, after=()):
    count, width = emb.shape
    sets = x.shape[0] // rows

    def kernel(*refs):
        refs = list(refs)
        held_ref = refs.pop(0) if held is not None else None
        emb_ref, x_ref = refs.pop(0), refs.pop(0)
        p_ref = refs.pop(0) if emb_p is not None else None
        before_ref = refs.pop(0) if before is not None else None
        del refs[: len(after)]
        out, stats, state = refs[0], refs[1], refs[-1]
        step = pl.program_id(0)

        def fold(s):
            groups = [s[:, i : i + 128] for i in range(0, s.shape[1], 128)]
            old = state[:, :128]
            top = functools.reduce(jnp.maximum, groups, old)
            total = state[:, 128:] * jnp.exp(old - top)
            state[:, :128] = top
            state[:, 128:] = total + sum(jnp.exp(g - top) for g in groups)

        @pl.when(step == 0)
        def _():
            if before is not None:
                state[...] = before_ref[...]
            else:
                state[:, :128] = jnp.full((count, 128), NEG_BIG, F32)
                state[:, 128:] = jnp.zeros((count, 128), F32)
            if emb_p is not None:
                inner = dot_t(emb_ref[...], p_ref[...]) * scale
                refs[2][...] = inner
                fold(inner)

        s = dot_t(emb_ref[...], x_ref[...]) * scale
        if held is not None:
            col = lax.broadcasted_iota(jnp.int32, s.shape, 1)
            s = jnp.where(col < held_ref[step], s, NEG_BIG)
        out[...] = s
        fold(s)

        @pl.when(step == sets - 1)
        def _():
            if pack:
                tops = state[:, :128].T
                top = jnp.max(tops, axis=0, keepdims=True)
                total = jnp.sum(state[:, 128:].T * jnp.exp(tops - top), axis=0, keepdims=True)
                row = lax.broadcasted_iota(jnp.int32, (8, count), 0)
                stats[...] = jnp.where(row == 0, top, total)
            else:
                stats[...] = state[...]

    whole = lambda a: pl.BlockSpec(a.shape, lambda i: (0, 0))
    args, in_specs = [emb, x], [whole(emb), pl.BlockSpec((rows, width), lambda i: (i, 0))]
    for a in (emb_p, before):
        if a is not None:
            args.append(a)
            in_specs.append(whole(a))
    args += after
    in_specs += [ANY] * len(after)
    if held is not None:
        args.insert(0, held)
        in_specs.insert(0, pl.BlockSpec(memory_space=pltpu.SMEM))
    stats_shape = (8, count) if pack else (count, 256)
    out_shape = [
        jax.ShapeDtypeStruct((count, x.shape[0]), F32),
        jax.ShapeDtypeStruct(stats_shape, F32),
    ]
    out_specs = [
        pl.BlockSpec((count, rows), lambda i: (0, i)),
        pl.BlockSpec(stats_shape, lambda i: (0, 0)),
    ]
    if emb_p is not None:
        out_shape.append(jax.ShapeDtypeStruct((count, count), F32))
        out_specs.append(pl.BlockSpec((count, count), lambda i: (0, 0)))
    return pl.pallas_call(
        kernel,
        grid=(sets,),
        in_specs=in_specs,
        out_specs=out_specs,
        out_shape=out_shape,
        scratch_shapes=[pltpu.VMEM((count, 256), F32)],
        compiler_params=params(),
        cost_estimate=pl.CostEstimate(
            flops=2 * count * x.shape[0] * width,
            bytes_accessed=2 * (count + x.shape[0]) * width,
            transcendentals=2 * count * x.shape[0],
        ),
        name="part_scores",
    )(*args)


def joined(mine, there):
    pad = jnp.zeros((120, mine.shape[1]), F32)
    m = jnp.concatenate([mine, pad], axis=0).T
    t = jnp.concatenate([there, pad], axis=0).T
    top = jnp.maximum(m[:, 0:1], t[:, 0:1])
    return top, m[:, 1:2] * jnp.exp(m[:, 0:1] - top) + t[:, 1:2] * jnp.exp(t[:, 0:1] - top)


def split_rows(x, cols):
    hi = x.astype(BF16).astype(F32)
    mid = (x - hi).astype(BF16).astype(F32)
    low = (x - hi - mid).astype(BF16).astype(F32)
    row = lax.broadcasted_iota(jnp.int32, (TAIL, cols), 0)
    wide = jnp.where(row == 0, hi, jnp.where(row == 1, mid, jnp.where(row == 2, low, 0.0)))
    return wide.astype(BF16)


def joined_rows(x):
    return jnp.sum(x[:, :128].astype(F32), axis=0, keepdims=True)[:, :1]


def guest_rows(mine, there, scores, guests, stays, scale, tile, after):
    count = mine.shape[1]
    n = len(guests)
    part, width = guests[0].shape
    tiles = width // tile

    def kernel(stays_ref, mine_ref, there_ref, *refs):
        s_refs, x_refs = refs[:n], refs[n : 2 * n]
        full, backs, probs = refs[2 * n + 1], refs[2 * n + 2 : -1], refs[-1]

        @pl.when(pl.program_id(0) == 0)
        def _():
            top, total = joined(mine_ref[...], there_ref[...])
            level = scale / total
            for k in range(n):
                probs[:, k * part : (k + 1) * part] = (
                    jnp.exp(s_refs[k][...] - top) * level
                ).astype(BF16)

        far = jnp.zeros((count, tile), F32)
        for k in range(n):
            far += jnp.dot(
                probs[:, k * part : (k + 1) * part], x_refs[k][...], preferred_element_type=F32
            )
        full[...] = far
        far = jnp.where(stays_ref[0] > 0, 0.0, far).astype(BF16)
        for i in range(tiles):

            @pl.when(pl.program_id(0) == i)
            def _():
                backs[i][...] = far

    whole = lambda a: pl.BlockSpec(a.shape, lambda i: (0, 0))
    return pl.pallas_call(
        kernel,
        grid=(tiles,),
        in_specs=[pl.BlockSpec(memory_space=pltpu.SMEM), whole(mine), whole(there)]
        + [whole(s) for s in scores]
        + [pl.BlockSpec((part, tile), lambda i: (0, i))] * n
        + [ANY],
        out_specs=[pl.BlockSpec((count, tile), lambda i: (0, i))]
        + [pl.BlockSpec((count, tile), lambda i: (0, 0))] * tiles,
        out_shape=[jax.ShapeDtypeStruct((count, width), F32)]
        + [jax.ShapeDtypeStruct((count, tile), BF16)] * tiles,
        scratch_shapes=[pltpu.VMEM((count, n * part), BF16)],
        compiler_params=params(),
        cost_estimate=pl.CostEstimate(
            flops=2 * count * n * part * width,
            bytes_accessed=2 * n * part * width + 6 * count * width,
            transcendentals=count * n * part,
        ),
        name="guest_rows",
    )(stays, mine, there, *scores, *guests, after)


def own_grads(mine, there, inner, own, scale):
    count = inner.shape[0]

    def kernel(mine_ref, there_ref, inner_ref, own_ref, out, near, near_t, loss):
        top, total = joined(mine_ref[...], there_ref[...])
        out[...] = (jnp.exp(own_ref[...] - top) * (scale / total)).astype(BF16)
        s = inner_ref[...]
        row = lax.broadcasted_iota(jnp.int32, s.shape, 0)
        col = lax.broadcasted_iota(jnp.int32, s.shape, 1)
        target = jnp.where(row == col, 1.0, 0.0)
        grad = (jnp.exp(s - top) / total - target) * scale
        near[...] = grad.astype(BF16)
        near_t[...] = grad.T.astype(BF16)
        rows = top + jnp.log(total) - jnp.sum(s * target, axis=1, keepdims=True)
        loss[...] = jnp.broadcast_to(jnp.sum(rows, axis=0, keepdims=True), loss.shape)

    wide = jax.ShapeDtypeStruct(own.shape, BF16)
    square = jax.ShapeDtypeStruct((count, count), BF16)
    return pl.pallas_call(
        kernel,
        out_shape=[wide, square, square, jax.ShapeDtypeStruct((8, 128), F32)],
        compiler_params=params(),
        cost_estimate=pl.CostEstimate(
            flops=8 * count * (own.shape[1] + count),
            bytes_accessed=6 * count * (own.shape[1] + count),
            transcendentals=count * (own.shape[1] + count),
        ),
        name="own_grads",
    )(mine, there, inner, own)


def grad_rows(p_own, near, near_t, own, emb_q, emb_p, far, backs, loss, stays, tile, start, before):
    count = near.shape[0]
    tiles = len(backs)
    total, width = own.shape

    def kernel(stays_ref, own_ref, near_ref, near_t_ref, x_ref, q_ref, p_ref, far_ref, *refs):
        back_refs, loss_ref = refs[:tiles], refs[tiles]
        outs, full = refs[-tiles - 1 : -1], refs[-1]
        acc = jnp.dot(near_ref[...], p_ref[...], preferred_element_type=F32)
        acc += jnp.dot(own_ref[...], x_ref[...], preferred_element_type=F32)
        acc += jnp.where(stays_ref[0] > 0, far_ref[...], 0.0)
        full[...] = acc
        pos = jnp.dot(near_t_ref[...], q_ref[...], preferred_element_type=F32).astype(BF16)
        acc = acc.astype(BF16)
        tail = split_rows(loss_ref[0:1, 0:1], tile)
        for i in range(tiles):

            @pl.when(pl.program_id(0) == i)
            def _():
                outs[i][:count] = acc
                outs[i][count : 2 * count] = pos
                outs[i][2 * count : 3 * count] = back_refs[i][...]
                outs[i][3 * count :] = tail

    whole = lambda a: pl.BlockSpec(a.shape, lambda i: (0, 0))
    cut = lambda r: pl.BlockSpec((r, tile), lambda i: (0, start + i))
    args = [stays, p_own, near, near_t, own, emb_q, emb_p, far, *backs, loss, *before]
    return pl.pallas_call(
        kernel,
        grid=(tiles,),
        in_specs=[pl.BlockSpec(memory_space=pltpu.SMEM)]
        + [whole(p_own), whole(near), whole(near_t), cut(total)]
        + [cut(count)] * 3
        + [whole(b) for b in backs]
        + [whole(loss)]
        + [ANY] * len(before),
        out_specs=[pl.BlockSpec((3 * count + TAIL, tile), lambda i: (0, 0))] * tiles
        + [cut(count)],
        out_shape=[jax.ShapeDtypeStruct((3 * count + TAIL, tile), BF16)] * tiles
        + [jax.ShapeDtypeStruct((count, width), F32)],
        input_output_aliases={len(args) - len(before) + i: tiles + i for i in range(len(before))},
        compiler_params=params(),
        cost_estimate=pl.CostEstimate(
            flops=2 * count * (total + 2 * count) * tile * tiles,
            bytes_accessed=(2 * total + 20 * count) * tile * tiles,
            transcendentals=0,
        ),
        name="grad_rows",
    )(*args)


def last_product(pieces, at, count, weight, tile, full=None, after=()):
    kin, width = weight.shape
    n = len(pieces)
    cols = pieces[0].shape[1]

    def kernel(w_ref, *refs):
        out, rows = refs[-2], refs[-1]

        @pl.when(pl.program_id(0) == 0)
        def _():
            for k in range(n):
                piece = refs[k][...]
                if full is not None:
                    piece = refs[n][:, k * cols : (k + 1) * cols] + piece.astype(F32)
                rows[:, k * cols : (k + 1) * cols] = piece.astype(BF16)

        out[...] = dot_t(rows[...], w_ref[...]).astype(BF16)

    args = [weight, *pieces]
    in_specs = [pl.BlockSpec((tile, width), lambda i: (i, 0))]
    in_specs += [pl.BlockSpec((count, cols), lambda i: (at, 0))] * n
    if full is not None:
        args.append(full)
        in_specs.append(pl.BlockSpec((count, width), lambda i: (0, 0)))
    return pl.pallas_call(
        kernel,
        grid=(kin // tile,),
        in_specs=in_specs + [ANY] * len(after),
        out_specs=pl.BlockSpec((count, tile), lambda i: (0, i)),
        out_shape=jax.ShapeDtypeStruct((count, kin), BF16),
        scratch_shapes=[pltpu.VMEM((count, width), BF16)],
        compiler_params=params(),
        cost_estimate=pl.CostEstimate(
            flops=2 * count * width * kin,
            bytes_accessed=2 * width * kin + 4 * count * (width + kin),
            transcendentals=0,
        ),
        name="last_product",
    )(*args, *after)


def weight_part(left, at, rights, base, rows_at, dtype, tails=(), after=()):
    depth, tile = left.shape[1], rights[0].shape[1]
    n, m = len(rights), len(rows_at)
    quarter = left.shape[0] // (8 if at is not None else 4)
    at = at or 0
    first, step = rows_at[0], rows_at[1] - rows_at[0]
    total = m * quarter

    def kernel(left_ref, *refs):
        out = refs[-2] if tails else refs[-1]
        if tails:
            rows = pl.ds(pl.multiple_of(pl.program_id(0) * quarter, quarter), quarter)
        else:
            rows = slice(None)
        for k in range(n):
            cols = slice(k * tile, (k + 1) * tile)
            acc = jnp.dot(left_ref[...], refs[k][...], preferred_element_type=F32)
            if base is not None:
                acc += refs[n][:, cols]
            out[rows, cols] = acc.astype(dtype)
        if tails:
            loss = sum(joined_rows(r[...]) for r in refs[n + 1 : n + 1 + len(tails)])
            out[total:, :] = split_rows(loss, n * tile)
            refs[-1][...] = jnp.broadcast_to(loss, refs[-1].shape)

    in_specs = [pl.BlockSpec((quarter, depth), lambda i: (at + first + step * i, 0))]
    in_specs += [pl.BlockSpec((depth, tile), lambda i: (0, 0))] * n
    args = [left, *rights]
    if base is not None:
        in_specs.append(pl.BlockSpec((quarter, n * tile), lambda i: (first + step * i, 0)))
        args.append(base)
    for t in tails:
        in_specs.append(pl.BlockSpec((TAIL, tile), lambda i: (depth // TAIL, 0)))
        args.append(t)
    in_specs += [ANY] * len(after)
    args += after
    if tails:
        shape = (total + TAIL, n * tile)
        out_shape = [jax.ShapeDtypeStruct(shape, dtype), jax.ShapeDtypeStruct((8, 128), F32)]
        out_specs = [pl.BlockSpec(s.shape, lambda i: (0, 0)) for s in out_shape]
    else:
        out_shape = jax.ShapeDtypeStruct((total, n * tile), dtype)
        out_specs = pl.BlockSpec((quarter, n * tile), lambda i: (i, 0))
    return pl.pallas_call(
        kernel,
        grid=(m,),
        in_specs=in_specs,
        out_specs=out_specs,
        out_shape=out_shape,
        compiler_params=params(),
        cost_estimate=pl.CostEstimate(
            flops=2 * total * n * depth * tile,
            bytes_accessed=2 * depth * (n * tile + total) + 8 * total * n * tile,
            transcendentals=0,
        ),
        name="weight_part",
    )(*args)


def fold_stage(keep, got, loss=None, after=(), outer=1):
    rows, cols = keep.shape
    mid = rows // 2

    def kernel(keep_ref, got_ref, *refs):
        if loss is None:
            send, rest = refs[-2:]
        else:
            send, rest, state = refs[-3:]
            value = refs[0][0:1, 0:1] + joined_rows(got_ref[rows:])
            state[...] = jnp.broadcast_to(value, state.shape)
            send[mid:] = split_rows(value, cols)
        part = mid // outer
        for o in range(outer):
            to = slice(o * part, (o + 1) * part)
            one = slice(2 * o * part, (2 * o + 1) * part)
            two = slice((2 * o + 1) * part, (2 * o + 2) * part)
            send[to] = (keep_ref[one] + got_ref[one].astype(F32)).astype(BF16)
            rest[to] = keep_ref[two] + got_ref[two].astype(F32)

    args = [keep, got] + ([loss] if loss is not None else [])
    in_specs = [pl.BlockSpec(memory_space=pltpu.VMEM)] * len(args)
    args += after
    in_specs += [ANY] * len(after)
    out_shape = [
        jax.ShapeDtypeStruct((mid + (TAIL if loss is not None else 0), cols), BF16),
        jax.ShapeDtypeStruct((rows - mid, cols), F32),
    ]
    if loss is not None:
        out_shape.append(jax.ShapeDtypeStruct((8, 128), F32))
    return pl.pallas_call(
        kernel,
        in_specs=in_specs,
        out_shape=out_shape,
        compiler_params=params(),
        cost_estimate=pl.CostEstimate(
            flops=rows * cols, bytes_accessed=9 * rows * cols, transcendentals=0
        ),
        name="fold_stage",
    )(*args)


def last_stage(keeps, gots, loss):
    rows, cols = keeps[0].shape

    def kernel(keep0, got0, keep1, got1, loss_ref, out, state):
        out[:, :cols] = keep0[...] + got0[:rows].astype(F32)
        out[:, cols:] = keep1[...] + got1[:rows].astype(F32)
        state[...] = loss_ref[...] + joined_rows(got0[rows:])

    return pl.pallas_call(
        kernel,
        out_shape=[
            jax.ShapeDtypeStruct((rows, 2 * cols), F32),
            jax.ShapeDtypeStruct((8, 128), F32),
        ],
        compiler_params=params(),
        name="last_stage",
    )(keeps[0], gots[0], keeps[1], gots[1], loss)


def body(queries, passages, weight, bank, neg_ids, block_home):
    count, kin = queries.shape
    width = weight.shape[1]
    scale = 1.0 / (SOFTMAX_TEMPER * math.sqrt(width))
    n_dp = lax.axis_size("dp")
    n_fsdp = lax.axis_size("fsdp")
    devices = n_dp * n_fsdp
    block_rows = bank.shape[1]
    named = neg_ids.shape[1]
    half = n_dp // 2
    me = lax.axis_index("dp")
    core = lax.axis_index("fsdp") % 2
    linear = me * n_fsdp + lax.axis_index("fsdp")

    trip = lambda f: half if f % 2 == 0 else 0

    ids = lax.all_to_all(
        jnp.broadcast_to(neg_ids, (n_dp, named)), "dp", split_axis=0, concat_axis=0, tiled=True
    )
    leaving = jnp.where(ids[0, 0] < 0, jnp.zeros_like(queries), queries)
    visit = move(leaving, trip)
    own, *guests, zero = pick_blocks(bank, ids, block_home, me, n_dp, n_fsdp)
    guests = [
        move(g, lambda f, k=k: k if f % 2 == 0 else k ^ half) for k, g in enumerate(guests)
    ]
    sides = [list(range(half)), list(range(half, n_dp))]
    own = lax.all_to_all(
        own, "dp", split_axis=0, concat_axis=0, tiled=True, axis_index_groups=sides
    )
    late = jnp.where(zero[0, 0] < 0, jnp.zeros_like(passages), passages)

    full_weight = lax.all_gather(weight, "fsdp", axis=0, tiled=True)
    emb_q = jnp.dot(queries, full_weight, preferred_element_type=F32).astype(BF16)
    emb_p = jnp.dot(passages, full_weight, preferred_element_type=F32).astype(BF16)
    emb_v = jnp.dot(visit, full_weight, preferred_element_type=F32).astype(BF16)

    f_bits = [("fsdp", b) for b in bits_of(n_fsdp)]
    d_bits = [("dp", b) for b in bits_of(n_dp)]
    stages = [f_bits[1], d_bits[0]] + f_bits[2:] + d_bits[1:]
    mask = []
    for p in range(devices // 2):
        m = 0
        for s, (axis, bit) in enumerate(stages):
            if not (p >> (len(stages) - 1 - s)) & 1:
                m |= bit if axis == "fsdp" else bit * n_fsdp
        mask.append(m)
    mask = jnp.array(mask, jnp.int32)
    hidden_t = jnp.concatenate([queries, late, visit], axis=0).T
    hidden_t = hidden_t.reshape(devices, kin // devices, -1)
    order = linear ^ jnp.concatenate([mask ^ 1, mask])
    left = jnp.take(hidden_t, order, axis=0).reshape(kin, -1)
    left_in = swap(left[: kin // 2], *f_bits[0])

    masked = n_dp * CAP > named
    own_held, guest_held = None, [None] * half
    if masked:
        owner = block_home[ids] // bank.shape[0] // n_fsdp
        held = lambda g, by: (jnp.sum(owner[g] == by) * block_rows).astype(jnp.int32)
        far = jnp.where(core == 0, 0, half)
        own_held = jnp.stack([held(me, (me & half) + k) for k in range(half)])
        guest_held = [held(me ^ half ^ far, me ^ k ^ far).reshape(1) for k in range(half)]
    rows = CAP * block_rows
    s_own, own_stats, inner = part_scores(
        emb_q, own, rows, own_held, scale, emb_p=emb_p, pack=True
    )
    their_stats = move(own_stats, trip)
    s_guest, stats = [], None
    for k, x in enumerate(guests):
        after = (inner,) if k == half // 2 else ()
        s, stats = part_scores(
            emb_v, x, rows, guest_held[k], scale, before=stats, pack=k == half - 1, after=after
        )
        s_guest.append(s)

    far_stats = move(stats, trip)
    tile = width // 4
    stays = core.astype(jnp.int32).reshape(1)
    far, *backs = guest_rows(
        stats, their_stats, s_guest, guests, stays, scale, tile, left_in
    )
    home = [move(r, trip) for r in backs]
    p_own, near, near_t, loss = own_grads(own_stats, far_stats, inner, s_own, scale)
    rows, kept = [], ()
    for i in range(2):
        *g, full = grad_rows(
            p_own,
            near,
            near_t,
            own,
            emb_q,
            emb_p,
            far,
            backs[2 * i : 2 * i + 2],
            loss,
            stays,
            tile,
            2 * i,
            kept,
        )
        rows += g
        kept = (full,)
    far_rows = [swap(r, *f_bits[0]) for r in rows]

    orders = [stages, [stages[1]] + d_bits[1:] + [stages[0]] + f_bits[2:]]
    lie = [stages[0]] + stages[2:]
    give = ((0, 1), (0, 2))
    hold = ((2, 3), (1, 3))
    every = (0, 1, 2, 3)
    bases = [
        weight_part(left, 4, rows[:2], None, every, F32),
        weight_part(left, 4, rows[2:], None, every, F32, after=(home[0],)),
    ]
    got = [far_rows[:2], far_rows[2:]]
    send, loss = weight_part(
        left_in, None, got[0], bases[0], give[0], BF16, tails=(rows[0], far_rows[0])
    )
    sends = [send, weight_part(left_in, None, got[1], bases[1], give[1], BF16, after=(home[1],))]
    back_p = last_product(rows, 1, count, full_weight, tile, after=(sends[1],))
    keeps = [
        weight_part(left_in, None, got[0], bases[0], hold[0], F32),
        weight_part(left_in, None, got[1], bases[1], hold[1], F32),
    ]
    waits = {(0, 0): (back_p, keeps[1]), (0, 1): (home[2], home[3])}
    for s in range(len(stages)):
        gots = [swap(sends[i], *orders[i][s]) for i in range(2)]
        if s + 1 < len(stages):
            send0, keep0, loss = fold_stage(keeps[0], gots[0], loss, waits.get((s, 0), ()))
            outer = 1 << lie.index(orders[1][s + 1])
            lie.remove(orders[1][s + 1])
            send1, keep1 = fold_stage(keeps[1], gots[1], after=waits.get((s, 1), ()), outer=outer)
            sends, keeps = [send0, send1], [keep0, keep1]
    back_q = last_product(home, 0, count, full_weight, tile, full=full, after=tuple(sends))
    grad_weight, loss = last_stage(keeps, gots, loss)
    loss = loss[0, 0] / (count * devices)
    return (loss, grad_weight, back_q, back_p)


def solution(mesh):
    return jax.shard_map(
        body,
        mesh=mesh,
        in_specs=(
            P(("dp", "fsdp"), None),
            P(("dp", "fsdp"), None),
            P("fsdp", None),
            P(("dp", "fsdp"), None, None),
            P(("dp", "fsdp"), None),
            P(),
        ),
        out_specs=(P(), P(("dp", "fsdp"), None), P(("dp", "fsdp"), None), P(("dp", "fsdp"), None)),
        check_vma=False,
    )
```

```python
import functools
import math

import jax
import jax.numpy as jnp
from jax import lax
from jax.experimental import pallas as pl
from jax.experimental.pallas import tpu as pltpu
from jax.sharding import PartitionSpec as P

CAP = 2

SOFTMAX_TEMPER = 0.25

NEG_BIG = -1e30

TAIL = 16

F32 = jnp.float32
BF16 = jnp.bfloat16

VMEM_LIMIT = 20 * 1024 * 1024


def bits_of(size):
    return [1 << i for i in range(size.bit_length() - 1)]


def swap(x, axis, bit):
    return lax.ppermute(x, axis, [(i, i ^ bit) for i in range(lax.axis_size(axis))])


def move(x, bit_of, stay=True):
    n_dp, n_fsdp = lax.axis_size("dp"), lax.axis_size("fsdp")
    pairs = [
        (i * n_fsdp + f, (i ^ bit_of(f)) * n_fsdp + f)
        for i in range(n_dp)
        for f in range(n_fsdp)
        if stay or bit_of(f)
    ]
    return lax.ppermute(x, ("dp", "fsdp"), pairs)


def dot_t(a, b):
    return lax.dot_general(a, b, (((1,), (1,)), ((), ())), preferred_element_type=F32)


ANY = pl.BlockSpec(memory_space=pl.ANY)


def params(**kw):
    return pltpu.CompilerParams(vmem_limit_bytes=VMEM_LIMIT, **kw)


def pick_blocks(bank, ids, block_home, me, n_dp, n_fsdp):
    per_dev, block_rows, width = bank.shape
    named = ids.shape[1]
    span = per_dev * n_fsdp
    half = n_dp // 2
    rows = CAP * block_rows

    def kernel(ids_ref, home_ref, me_ref, bank_ref, own, *refs):
        guests, none, table, held, sem, whole_sem = refs[:half], *refs[half:]
        load = pltpu.make_async_copy(bank_ref, held, whole_sem)
        load.start()
        here = me_ref[0]
        none[...] = jnp.zeros(none.shape, none.dtype)
        base = here & half
        targets = [(here ^ k ^ half, guests[k], 0) for k in range(half)]
        targets += [(base + k, own, k * rows) for k in range(half)]
        for t, (group, _, _) in enumerate(targets):
            for p in range(CAP):
                table[t * CAP + p] = 0
            count = jnp.int32(0)
            for j in range(named):
                slot = home_ref[ids_ref[group, j]]
                mine = lax.div(slot, span) == here

                @pl.when(mine)
                def _():
                    table[t * CAP + jnp.minimum(count, CAP - 1)] = lax.rem(slot, per_dev)

                count = count + mine.astype(jnp.int32)
        load.wait()
        copies = []
        for t, (_, out, at) in enumerate(targets):
            for p in range(CAP):
                copy = pltpu.make_async_copy(
                    held.at[table[t * CAP + p]],
                    out.at[pl.ds(at + p * block_rows, block_rows)],
                    sem.at[len(copies)],
                )
                copy.start()
                copies.append(copy)
        for copy in copies:
            copy.wait()

    smem = pl.BlockSpec(memory_space=pltpu.SMEM)
    return pl.pallas_call(
        kernel,
        in_specs=[smem, smem, smem, ANY],
        out_specs=[ANY] * (half + 1) + [pl.BlockSpec(memory_space=pltpu.VMEM)],
        out_shape=[jax.ShapeDtypeStruct((half * rows, width), bank.dtype)]
        + [jax.ShapeDtypeStruct((rows, width), bank.dtype)] * half
        + [jax.ShapeDtypeStruct((8, 128), jnp.int32)],
        scratch_shapes=[
            pltpu.SMEM((n_dp * CAP,), jnp.int32),
            pltpu.VMEM(bank.shape, bank.dtype),
            pltpu.SemaphoreType.DMA((n_dp * CAP,)),
            pltpu.SemaphoreType.DMA,
        ],
        compiler_params=params(),
        cost_estimate=pl.CostEstimate(
            flops=0, bytes_accessed=4 * n_dp * rows * width, transcendentals=0
        ),
        name="pick_blocks",
    )(ids, block_home, me.reshape(1), bank)


def part_scores(
    emb, count, x, rows, held, scale, near=False, before=None, pack=False, after=(), other=()
):
    width = emb.shape[1]
    sets = x.shape[0] // rows

    def kernel(*refs):
        refs = list(refs)
        held_ref = refs.pop(0) if held is not None else None
        emb_ref, x_ref = refs.pop(0), refs.pop(0)
        p_ref = refs.pop(0) if near else None
        before_ref = refs.pop(0) if before is not None else None
        other_refs = [refs.pop(0) for _ in other]
        del refs[: len(after)]
        out, stats, state = refs[0], refs[1], refs[-1]
        step = pl.program_id(0)

        def fold(s):
            groups = [s[:, i : i + 128] for i in range(0, s.shape[1], 128)]
            old = state[:, :128]
            top = functools.reduce(jnp.maximum, groups, old)
            total = state[:, 128:] * jnp.exp(old - top)
            state[:, :128] = top
            state[:, 128:] = total + sum(jnp.exp(g - top) for g in groups)

        @pl.when(step == 0)
        def _():
            if before is not None:
                state[...] = before_ref[...]
            else:
                state[:, :128] = jnp.full((count, 128), NEG_BIG, F32)
                state[:, 128:] = jnp.zeros((count, 128), F32)
            if near:
                inner = dot_t(emb_ref[...], p_ref[...]) * scale
                refs[2][...] = inner
                fold(inner)

        cand = x_ref[...]
        if other:
            cand = lax.select(other_refs[0][0] > 0, cand, other_refs[1][...])
        s = dot_t(emb_ref[...], cand) * scale
        if held is not None:
            col = lax.broadcasted_iota(jnp.int32, s.shape, 1)
            s = jnp.where(col < held_ref[step], s, NEG_BIG)
        out[...] = s
        fold(s)

        @pl.when(step == sets - 1)
        def _():
            if pack:
                tops = state[:, :128].T
                top = jnp.max(tops, axis=0, keepdims=True)
                total = jnp.sum(state[:, 128:].T * jnp.exp(tops - top), axis=0, keepdims=True)
                row = lax.broadcasted_iota(jnp.int32, (8, count), 0)
                stats[...] = jnp.where(row == 0, top, total)
            else:
                stats[...] = state[...]

    whole = lambda a: pl.BlockSpec(a.shape, lambda i: (0, 0))
    args = [emb, x]
    in_specs = [pl.BlockSpec((count, width), lambda i: (0, 0))]
    in_specs.append(pl.BlockSpec((rows, width), lambda i: (i, 0)))
    if near:
        args.append(emb)
        in_specs.append(pl.BlockSpec((count, width), lambda i: (1, 0)))
    if before is not None:
        args.append(before)
        in_specs.append(whole(before))
    if other:
        args += other
        in_specs.append(pl.BlockSpec(memory_space=pltpu.SMEM))
        in_specs.append(pl.BlockSpec((rows, width), lambda i: (i, 0)))
    args += after
    in_specs += [ANY] * len(after)
    if held is not None:
        args.insert(0, held)
        in_specs.insert(0, pl.BlockSpec(memory_space=pltpu.SMEM))
    stats_shape = (8, count) if pack else (count, 256)
    out_shape = [
        jax.ShapeDtypeStruct((count, x.shape[0]), F32),
        jax.ShapeDtypeStruct(stats_shape, F32),
    ]
    out_specs = [
        pl.BlockSpec((count, rows), lambda i: (0, i)),
        pl.BlockSpec(stats_shape, lambda i: (0, 0)),
    ]
    if near:
        out_shape.append(jax.ShapeDtypeStruct((count, count), F32))
        out_specs.append(pl.BlockSpec((count, count), lambda i: (0, 0)))
    return pl.pallas_call(
        kernel,
        grid=(sets,),
        in_specs=in_specs,
        out_specs=out_specs,
        out_shape=out_shape,
        scratch_shapes=[pltpu.VMEM((count, 256), F32)],
        compiler_params=params(),
        cost_estimate=pl.CostEstimate(
            flops=2 * count * x.shape[0] * width,
            bytes_accessed=2 * (count + x.shape[0]) * width,
            transcendentals=2 * count * x.shape[0],
        ),
        name="part_scores",
    )(*args)


def joined(mine, there):
    pad = jnp.zeros((120, mine.shape[1]), F32)
    m = jnp.concatenate([mine, pad], axis=0).T
    t = jnp.concatenate([there, pad], axis=0).T
    top = jnp.maximum(m[:, 0:1], t[:, 0:1])
    return top, m[:, 1:2] * jnp.exp(m[:, 0:1] - top) + t[:, 1:2] * jnp.exp(t[:, 0:1] - top)


def split_rows(x, cols):
    hi = x.astype(BF16).astype(F32)
    mid = (x - hi).astype(BF16).astype(F32)
    low = (x - hi - mid).astype(BF16).astype(F32)
    row = lax.broadcasted_iota(jnp.int32, (TAIL, cols), 0)
    wide = jnp.where(row == 0, hi, jnp.where(row == 1, mid, jnp.where(row == 2, low, 0.0)))
    return wide.astype(BF16)


def joined_rows(x):
    return jnp.sum(x[:, :128].astype(F32), axis=0, keepdims=True)[:, :1]


def guest_rows(mine, there, scores, guests, stay, stays, scale, tile, after):
    count = mine.shape[1]
    n = len(guests)
    part, width = guests[0].shape
    tiles = width // tile

    def kernel(stays_ref, mine_ref, there_ref, *refs):
        s_refs, x_refs = refs[:n], refs[n : 2 * n]
        stay_ref, full, backs, probs = refs[2 * n], refs[2 * n + 2], refs[2 * n + 3 : -1], refs[-1]

        @pl.when(pl.program_id(0) == 0)
        def _():
            top, total = joined(mine_ref[...], there_ref[...])
            level = scale / total
            for k in range(n):
                probs[:, k * part : (k + 1) * part] = (
                    jnp.exp(s_refs[k][...] - top) * level
                ).astype(BF16)

        far = jnp.zeros((count, tile), F32)
        for k in range(n):
            x = x_refs[k][...]
            if k == 0:
                x = lax.select(stays_ref[0] > 0, x, stay_ref[...])
            far += jnp.dot(
                probs[:, k * part : (k + 1) * part], x, preferred_element_type=F32
            )
        full[...] = far
        far = jnp.where(stays_ref[0] > 0, 0.0, far).astype(BF16)
        for i in range(tiles):

            @pl.when(pl.program_id(0) == i)
            def _():
                backs[i][...] = far

    whole = lambda a: pl.BlockSpec(a.shape, lambda i: (0, 0))
    return pl.pallas_call(
        kernel,
        grid=(tiles,),
        in_specs=[pl.BlockSpec(memory_space=pltpu.SMEM), whole(mine), whole(there)]
        + [whole(s) for s in scores]
        + [pl.BlockSpec((part, tile), lambda i: (0, i))] * (n + 1)
        + [ANY],
        out_specs=[pl.BlockSpec((count, tile), lambda i: (0, i))]
        + [pl.BlockSpec((count, tile), lambda i: (0, 0))] * tiles,
        out_shape=[jax.ShapeDtypeStruct((count, width), F32)]
        + [jax.ShapeDtypeStruct((count, tile), BF16)] * tiles,
        scratch_shapes=[pltpu.VMEM((count, n * part), BF16)],
        compiler_params=params(),
        cost_estimate=pl.CostEstimate(
            flops=2 * count * n * part * width,
            bytes_accessed=2 * n * part * width + 6 * count * width,
            transcendentals=count * n * part,
        ),
        name="guest_rows",
    )(stays, mine, there, *scores, *guests, stay, after)


def own_grads(mine, there, inner, own, scale):
    count = inner.shape[0]

    def kernel(mine_ref, there_ref, inner_ref, own_ref, out, near, near_t, loss):
        top, total = joined(mine_ref[...], there_ref[...])
        out[...] = (jnp.exp(own_ref[...] - top) * (scale / total)).astype(BF16)
        s = inner_ref[...]
        row = lax.broadcasted_iota(jnp.int32, s.shape, 0)
        col = lax.broadcasted_iota(jnp.int32, s.shape, 1)
        target = jnp.where(row == col, 1.0, 0.0)
        grad = (jnp.exp(s - top) / total - target) * scale
        near[...] = grad.astype(BF16)
        near_t[...] = grad.T.astype(BF16)
        rows = top + jnp.log(total) - jnp.sum(s * target, axis=1, keepdims=True)
        loss[...] = jnp.broadcast_to(jnp.sum(rows, axis=0, keepdims=True), loss.shape)

    wide = jax.ShapeDtypeStruct(own.shape, BF16)
    square = jax.ShapeDtypeStruct((count, count), BF16)
    return pl.pallas_call(
        kernel,
        out_shape=[wide, square, square, jax.ShapeDtypeStruct((8, 128), F32)],
        compiler_params=params(),
        cost_estimate=pl.CostEstimate(
            flops=8 * count * (own.shape[1] + count),
            bytes_accessed=6 * count * (own.shape[1] + count),
            transcendentals=count * (own.shape[1] + count),
        ),
        name="own_grads",
    )(mine, there, inner, own)


def grad_rows(p_own, near, near_t, own, emb, far, backs, loss, stays, tile, start, before):
    count = near.shape[0]
    tiles = len(backs)
    total, width = own.shape

    def kernel(stays_ref, own_ref, near_ref, near_t_ref, x_ref, q_ref, p_ref, far_ref, *refs):
        back_refs, loss_ref = refs[:tiles], refs[tiles]
        outs, full = refs[-tiles - 1 : -1], refs[-1]
        acc = jnp.dot(near_ref[...], p_ref[...], preferred_element_type=F32)
        acc += jnp.dot(own_ref[...], x_ref[...], preferred_element_type=F32)
        acc += jnp.where(stays_ref[0] > 0, far_ref[...], 0.0)
        full[...] = acc
        pos = jnp.dot(near_t_ref[...], q_ref[...], preferred_element_type=F32).astype(BF16)
        acc = acc.astype(BF16)
        tail = split_rows(loss_ref[0:1, 0:1], tile)
        for i in range(tiles):

            @pl.when(pl.program_id(0) == i)
            def _():
                outs[i][:count] = acc
                outs[i][count : 2 * count] = pos
                outs[i][2 * count : 3 * count] = back_refs[i][...]
                outs[i][3 * count :] = tail

    whole = lambda a: pl.BlockSpec(a.shape, lambda i: (0, 0))
    cut = lambda r, at=0: pl.BlockSpec((r, tile), lambda i: (at, start + i))
    args = [stays, p_own, near, near_t, own, emb, emb, far, *backs, loss, *before]
    return pl.pallas_call(
        kernel,
        grid=(tiles,),
        in_specs=[pl.BlockSpec(memory_space=pltpu.SMEM)]
        + [whole(p_own), whole(near), whole(near_t), cut(total)]
        + [cut(count), cut(count, 1), cut(count)]
        + [whole(b) for b in backs]
        + [whole(loss)]
        + [ANY] * len(before),
        out_specs=[pl.BlockSpec((3 * count + TAIL, tile), lambda i: (0, 0))] * tiles
        + [cut(count)],
        out_shape=[jax.ShapeDtypeStruct((3 * count + TAIL, tile), BF16)] * tiles
        + [jax.ShapeDtypeStruct((count, width), F32)],
        input_output_aliases={len(args) - len(before) + i: tiles + i for i in range(len(before))},
        compiler_params=params(),
        cost_estimate=pl.CostEstimate(
            flops=2 * count * (total + 2 * count) * tile * tiles,
            bytes_accessed=(2 * total + 20 * count) * tile * tiles,
            transcendentals=0,
        ),
        name="grad_rows",
    )(*args)


def last_product(pieces, at, count, weight, tile, full=None, after=()):
    kin, width = weight.shape
    n = len(pieces)
    cols = pieces[0].shape[1]

    def kernel(w_ref, *refs):
        out, rows = refs[-2], refs[-1]

        @pl.when(pl.program_id(0) == 0)
        def _():
            for k in range(n):
                piece = refs[k][...]
                if full is not None:
                    piece = refs[n][:, k * cols : (k + 1) * cols] + piece.astype(F32)
                rows[:, k * cols : (k + 1) * cols] = piece.astype(BF16)

        out[...] = dot_t(rows[...], w_ref[...]).astype(BF16)

    args = [weight, *pieces]
    in_specs = [pl.BlockSpec((tile, width), lambda i: (i, 0))]
    in_specs += [pl.BlockSpec((count, cols), lambda i: (at, 0))] * n
    if full is not None:
        args.append(full)
        in_specs.append(pl.BlockSpec((count, width), lambda i: (0, 0)))
    return pl.pallas_call(
        kernel,
        grid=(kin // tile,),
        in_specs=in_specs + [ANY] * len(after),
        out_specs=pl.BlockSpec((count, tile), lambda i: (0, i)),
        out_shape=jax.ShapeDtypeStruct((count, kin), BF16),
        scratch_shapes=[pltpu.VMEM((count, width), BF16)],
        compiler_params=params(),
        cost_estimate=pl.CostEstimate(
            flops=2 * count * width * kin,
            bytes_accessed=2 * width * kin + 4 * count * (width + kin),
            transcendentals=0,
        ),
        name="last_product",
    )(*args, *after)


def weight_part(left, at, rights, base, rows_at, dtype, tails=(), after=()):
    depth, tile = left.shape[1], rights[0].shape[1]
    n, m = len(rights), len(rows_at)
    quarter = left.shape[0] // (8 if at is not None else 4)
    at = at or 0
    first, step = rows_at[0], rows_at[1] - rows_at[0]
    total = m * quarter

    def kernel(left_ref, *refs):
        out = refs[-2] if tails else refs[-1]
        if tails:
            rows = pl.ds(pl.multiple_of(pl.program_id(0) * quarter, quarter), quarter)
        else:
            rows = slice(None)
        for k in range(n):
            cols = slice(k * tile, (k + 1) * tile)
            acc = jnp.dot(left_ref[...], refs[k][...], preferred_element_type=F32)
            if base is not None:
                acc += refs[n][:, cols]
            out[rows, cols] = acc.astype(dtype)
        if tails:
            loss = sum(joined_rows(r[...]) for r in refs[n + 1 : n + 1 + len(tails)])
            out[total:, :] = split_rows(loss, n * tile)
            refs[-1][...] = jnp.broadcast_to(loss, refs[-1].shape)

    in_specs = [pl.BlockSpec((quarter, depth), lambda i: (at + first + step * i, 0))]
    in_specs += [pl.BlockSpec((depth, tile), lambda i: (0, 0))] * n
    args = [left, *rights]
    if base is not None:
        in_specs.append(pl.BlockSpec((quarter, n * tile), lambda i: (first + step * i, 0)))
        args.append(base)
    for t in tails:
        in_specs.append(pl.BlockSpec((TAIL, tile), lambda i: (depth // TAIL, 0)))
        args.append(t)
    in_specs += [ANY] * len(after)
    args += after
    if tails:
        shape = (total + TAIL, n * tile)
        out_shape = [jax.ShapeDtypeStruct(shape, dtype), jax.ShapeDtypeStruct((8, 128), F32)]
        out_specs = [pl.BlockSpec(s.shape, lambda i: (0, 0)) for s in out_shape]
    else:
        out_shape = jax.ShapeDtypeStruct((total, n * tile), dtype)
        out_specs = pl.BlockSpec((quarter, n * tile), lambda i: (i, 0))
    return pl.pallas_call(
        kernel,
        grid=(m,),
        in_specs=in_specs,
        out_specs=out_specs,
        out_shape=out_shape,
        compiler_params=params(),
        cost_estimate=pl.CostEstimate(
            flops=2 * total * n * depth * tile,
            bytes_accessed=2 * depth * (n * tile + total) + 8 * total * n * tile,
            transcendentals=0,
        ),
        name="weight_part",
    )(*args)


def fold_stage(keep, got, loss=None, after=()):
    rows, cols = keep.shape
    mid = rows // 2

    def kernel(keep_ref, got_ref, *refs):
        if loss is None:
            send, rest = refs[-2:]
        else:
            send, rest, state = refs[-3:]
            value = refs[0][0:1, 0:1] + joined_rows(got_ref[rows:])
            state[...] = jnp.broadcast_to(value, state.shape)
            send[mid:] = split_rows(value, cols)
        send[:mid] = (keep_ref[:mid] + got_ref[:mid].astype(F32)).astype(BF16)
        rest[...] = keep_ref[mid:] + got_ref[mid:rows].astype(F32)

    args = [keep, got] + ([loss] if loss is not None else [])
    in_specs = [pl.BlockSpec(memory_space=pltpu.VMEM)] * len(args)
    args += after
    in_specs += [ANY] * len(after)
    out_shape = [
        jax.ShapeDtypeStruct((mid + (TAIL if loss is not None else 0), cols), BF16),
        jax.ShapeDtypeStruct((rows - mid, cols), F32),
    ]
    if loss is not None:
        out_shape.append(jax.ShapeDtypeStruct((8, 128), F32))
    return pl.pallas_call(
        kernel,
        in_specs=in_specs,
        out_shape=out_shape,
        compiler_params=params(),
        cost_estimate=pl.CostEstimate(
            flops=rows * cols, bytes_accessed=9 * rows * cols, transcendentals=0
        ),
        name="fold_stage",
    )(*args)


def last_stage(keeps, gots, loss):
    rows, cols = keeps[0].shape

    def kernel(keep0, got0, keep1, got1, loss_ref, out, state):
        out[:, :cols] = keep0[...] + got0[:rows].astype(F32)
        out[:, cols:] = keep1[...] + got1[:rows].astype(F32)
        state[...] = loss_ref[...] + joined_rows(got0[rows:])

    return pl.pallas_call(
        kernel,
        out_shape=[
            jax.ShapeDtypeStruct((rows, 2 * cols), F32),
            jax.ShapeDtypeStruct((8, 128), F32),
        ],
        compiler_params=params(),
        name="last_stage",
    )(keeps[0], gots[0], keeps[1], gots[1], loss)


def body(queries, passages, weight, bank, neg_ids, block_home):
    count, kin = queries.shape
    width = weight.shape[1]
    scale = 1.0 / (SOFTMAX_TEMPER * math.sqrt(width))
    n_dp = lax.axis_size("dp")
    n_fsdp = lax.axis_size("fsdp")
    devices = n_dp * n_fsdp
    block_rows = bank.shape[1]
    named = neg_ids.shape[1]
    half = n_dp // 2
    me = lax.axis_index("dp")
    core = lax.axis_index("fsdp") % 2
    linear = me * n_fsdp + lax.axis_index("fsdp")

    trip = lambda f: half if f % 2 == 0 else 0

    ids = lax.all_to_all(
        jnp.broadcast_to(neg_ids, (n_dp, named)), "dp", split_axis=0, concat_axis=0, tiled=True
    )
    leaving = jnp.where(ids[0, 0] < 0, jnp.zeros_like(queries), queries)
    visit = jnp.where(core == 0, move(leaving, trip, stay=False), queries)
    own, *guests, zero = pick_blocks(bank, ids, block_home, me, n_dp, n_fsdp)
    stay = guests[0]
    guests = [
        move(g, lambda f, k=k: k if f % 2 == 0 else k ^ half, stay=False)
        for k, g in enumerate(guests)
    ]
    stays = core.astype(jnp.int32).reshape(1)
    sides = [list(range(half)), list(range(half, n_dp))]
    own = lax.all_to_all(
        own, "dp", split_axis=0, concat_axis=0, tiled=True, axis_index_groups=sides
    )
    late = jnp.where(zero[0, 0] < 0, jnp.zeros_like(passages), passages)

    full_weight = lax.all_gather(weight, "fsdp", axis=0, tiled=True)
    both = jnp.concatenate([queries, passages], axis=0)
    emb = jnp.dot(both, full_weight, preferred_element_type=F32).astype(BF16)
    emb_v = jnp.dot(visit, full_weight, preferred_element_type=F32).astype(BF16)

    f_bits = [("fsdp", b) for b in bits_of(n_fsdp)]
    d_bits = [("dp", b) for b in bits_of(n_dp)]
    stages = [f_bits[1], d_bits[0]] + f_bits[2:] + d_bits[1:]
    mask = []
    for p in range(devices // 2):
        m = 0
        for s, (axis, bit) in enumerate(stages):
            if not (p >> (len(stages) - 1 - s)) & 1:
                m |= bit if axis == "fsdp" else bit * n_fsdp
        mask.append(m)
    mask = jnp.array(mask, jnp.int32)
    hidden_t = jnp.concatenate([queries, late, visit], axis=0).T
    hidden_t = hidden_t.reshape(devices, kin // devices, -1)
    order = linear ^ jnp.concatenate([mask ^ 1, mask])
    left = jnp.take(hidden_t, order, axis=0).reshape(kin, -1)
    left_in = swap(left[: kin // 2], *f_bits[0])

    masked = n_dp * CAP > named
    own_held, guest_held = None, [None] * half
    if masked:
        owner = block_home[ids] // bank.shape[0] // n_fsdp
        held = lambda g, by: (jnp.sum(owner[g] == by) * block_rows).astype(jnp.int32)
        far = jnp.where(core == 0, 0, half)
        own_held = jnp.stack([held(me, (me & half) + k) for k in range(half)])
        guest_held = [held(me ^ half ^ far, me ^ k ^ far).reshape(1) for k in range(half)]
    rows = CAP * block_rows
    s_own, own_stats, inner = part_scores(
        emb, count, own, rows, own_held, scale, near=True, pack=True
    )
    their_stats = move(own_stats, trip)
    s_guest, stats = [], None
    for k, x in enumerate(guests):
        after = (inner,) if k == half // 2 else ()
        s, stats = part_scores(
            emb_v,
            count,
            x,
            rows,
            guest_held[k],
            scale,
            before=stats,
            pack=k == half - 1,
            after=after,
            other=(stays, stay) if k == 0 else (),
        )
        s_guest.append(s)

    far_stats = move(stats, trip)
    tile = width // 4
    far, *backs = guest_rows(
        stats, their_stats, s_guest, guests, stay, stays, scale, tile, left_in
    )
    home = [move(r, trip) for r in backs]
    p_own, near, near_t, loss = own_grads(own_stats, far_stats, inner, s_own, scale)
    rows, kept = [], ()
    for i in range(2):
        *g, full = grad_rows(
            p_own,
            near,
            near_t,
            own,
            emb,
            far,
            backs[2 * i : 2 * i + 2],
            loss,
            stays,
            tile,
            2 * i,
            kept,
        )
        rows += g
        kept = (full,)
    far_rows = [swap(r, *f_bits[0]) for r in rows]

    orders = [stages, [stages[1], stages[0]] + stages[2:]]
    give = ((0, 1), (0, 2))
    hold = ((2, 3), (1, 3))
    every = (0, 1, 2, 3)
    bases = [
        weight_part(left, 4, rows[:2], None, every, F32),
        weight_part(left, 4, rows[2:], None, every, F32, after=(home[0],)),
    ]
    got = [far_rows[:2], far_rows[2:]]
    send, loss = weight_part(
        left_in, None, got[0], bases[0], give[0], BF16, tails=(rows[0], far_rows[0])
    )
    sends = [send, weight_part(left_in, None, got[1], bases[1], give[1], BF16, after=(home[1],))]
    back_p = last_product(rows, 1, count, full_weight, tile, after=(sends[1],))
    keeps = [
        weight_part(left_in, None, got[0], bases[0], hold[0], F32),
        weight_part(left_in, None, got[1], bases[1], hold[1], F32),
    ]
    waits = {(0, 0): (back_p, keeps[1]), (0, 1): (home[2], home[3])}
    for s in range(len(stages)):
        gots = [swap(sends[i], *orders[i][s]) for i in range(2)]
        if s + 1 < len(stages):
            send0, keep0, loss = fold_stage(keeps[0], gots[0], loss, waits.get((s, 0), ()))
            send1, keep1 = fold_stage(keeps[1], gots[1], after=waits.get((s, 1), ()))
            sends, keeps = [send0, send1], [keep0, keep1]
    back_q = last_product(home, 0, count, full_weight, tile, full=full, after=tuple(sends))
    grad_weight, loss = last_stage(keeps, gots, loss)
    loss = loss[0, 0] / (count * devices)
    return (loss, grad_weight, back_q, back_p)


def solution(mesh):
    return jax.shard_map(
        body,
        mesh=mesh,
        in_specs=(
            P(("dp", "fsdp"), None),
            P(("dp", "fsdp"), None),
            P("fsdp", None),
            P(("dp", "fsdp"), None, None),
            P(("dp", "fsdp"), None),
            P(),
        ),
        out_specs=(P(), P(("dp", "fsdp"), None), P(("dp", "fsdp"), None), P(("dp", "fsdp"), None)),
        check_vma=False,
    )
```

```python
import functools
import math

import jax
import jax.numpy as jnp
from jax import lax
from jax.experimental import pallas as pl
from jax.experimental.pallas import tpu as pltpu
from jax.sharding import PartitionSpec as P

CAP = 2

SOFTMAX_TEMPER = 0.25

NEG_BIG = -1e30

TAIL = 16

F32 = jnp.float32
BF16 = jnp.bfloat16

VMEM_LIMIT = 20 * 1024 * 1024


def bits_of(size):
    return [1 << i for i in range(size.bit_length() - 1)]


def swap(x, axis, bit):
    return lax.ppermute(x, axis, [(i, i ^ bit) for i in range(lax.axis_size(axis))])


def move(x, bit_of):
    n_dp, n_fsdp = lax.axis_size("dp"), lax.axis_size("fsdp")
    pairs = [
        (i * n_fsdp + f, (i ^ bit_of(f)) * n_fsdp + f) for i in range(n_dp) for f in range(n_fsdp)
    ]
    return lax.ppermute(x, ("dp", "fsdp"), pairs)


def dot_t(a, b):
    return lax.dot_general(a, b, (((1,), (1,)), ((), ())), preferred_element_type=F32)


ANY = pl.BlockSpec(memory_space=pl.ANY)


def params(**kw):
    return pltpu.CompilerParams(vmem_limit_bytes=VMEM_LIMIT, **kw)


def pick_blocks(bank, ids, block_home, me, n_dp, n_fsdp):
    per_dev, block_rows, width = bank.shape
    named = ids.shape[1]
    span = per_dev * n_fsdp
    half = n_dp // 2
    rows = CAP * block_rows

    def kernel(ids_ref, home_ref, me_ref, bank_ref, own, *refs):
        guests, none, table, held, sem, whole_sem = refs[:half], *refs[half:]
        load = pltpu.make_async_copy(bank_ref, held, whole_sem)
        load.start()
        here = me_ref[0]
        none[...] = jnp.zeros(none.shape, none.dtype)
        base = here & half
        targets = [(here ^ k ^ half, guests[k], 0) for k in range(half)]
        targets += [(base + k, own, k * rows) for k in range(half)]
        for t, (group, _, _) in enumerate(targets):
            for p in range(CAP):
                table[t * CAP + p] = 0
            count = jnp.int32(0)
            for j in range(named):
                slot = home_ref[ids_ref[group, j]]
                mine = lax.div(slot, span) == here

                @pl.when(mine)
                def _():
                    table[t * CAP + jnp.minimum(count, CAP - 1)] = lax.rem(slot, per_dev)

                count = count + mine.astype(jnp.int32)
        load.wait()
        copies = []
        for t, (_, out, at) in enumerate(targets):
            for p in range(CAP):
                copy = pltpu.make_async_copy(
                    held.at[table[t * CAP + p]],
                    out.at[pl.ds(at + p * block_rows, block_rows)],
                    sem.at[len(copies)],
                )
                copy.start()
                copies.append(copy)
        for copy in copies:
            copy.wait()

    smem = pl.BlockSpec(memory_space=pltpu.SMEM)
    return pl.pallas_call(
        kernel,
        in_specs=[smem, smem, smem, ANY],
        out_specs=[ANY] * (half + 1) + [pl.BlockSpec(memory_space=pltpu.VMEM)],
        out_shape=[jax.ShapeDtypeStruct((half * rows, width), bank.dtype)]
        + [jax.ShapeDtypeStruct((rows, width), bank.dtype)] * half
        + [jax.ShapeDtypeStruct((8, 128), jnp.int32)],
        scratch_shapes=[
            pltpu.SMEM((n_dp * CAP,), jnp.int32),
            pltpu.VMEM(bank.shape, bank.dtype),
            pltpu.SemaphoreType.DMA((n_dp * CAP,)),
            pltpu.SemaphoreType.DMA,
        ],
        compiler_params=params(),
        cost_estimate=pl.CostEstimate(
            flops=0, bytes_accessed=4 * n_dp * rows * width, transcendentals=0
        ),
        name="pick_blocks",
    )(ids, block_home, me.reshape(1), bank)


def part_scores(emb, x, rows, held, scale, emb_p=None, before=None, pack=False, after=()):
    count, width = emb.shape
    sets = x.shape[0] // rows

    def kernel(*refs):
        refs = list(refs)
        held_ref = refs.pop(0) if held is not None else None
        emb_ref, x_ref = refs.pop(0), refs.pop(0)
        p_ref = refs.pop(0) if emb_p is not None else None
        before_ref = refs.pop(0) if before is not None else None
        del refs[: len(after)]
        out, stats, state = refs[0], refs[1], refs[-1]
        step = pl.program_id(0)

        def fold(s):
            groups = [s[:, i : i + 128] for i in range(0, s.shape[1], 128)]
            old = state[:, :128]
            top = functools.reduce(jnp.maximum, groups, old)
            total = state[:, 128:] * jnp.exp(old - top)
            state[:, :128] = top
            state[:, 128:] = total + sum(jnp.exp(g - top) for g in groups)

        @pl.when(step == 0)
        def _():
            if before is not None:
                state[...] = before_ref[...]
            else:
                state[:, :128] = jnp.full((count, 128), NEG_BIG, F32)
                state[:, 128:] = jnp.zeros((count, 128), F32)
            if emb_p is not None:
                inner = dot_t(emb_ref[...], p_ref[...]) * scale
                refs[2][...] = inner
                fold(inner)

        s = dot_t(emb_ref[...], x_ref[...]) * scale
        if held is not None:
            col = lax.broadcasted_iota(jnp.int32, s.shape, 1)
            s = jnp.where(col < held_ref[step], s, NEG_BIG)
        out[...] = s
        fold(s)

        @pl.when(step == sets - 1)
        def _():
            if pack:
                tops = state[:, :128].T
                top = jnp.max(tops, axis=0, keepdims=True)
                total = jnp.sum(state[:, 128:].T * jnp.exp(tops - top), axis=0, keepdims=True)
                row = lax.broadcasted_iota(jnp.int32, (8, count), 0)
                stats[...] = jnp.where(row == 0, top, total)
            else:
                stats[...] = state[...]

    whole = lambda a: pl.BlockSpec(a.shape, lambda i: (0, 0))
    args, in_specs = [emb, x], [whole(emb), pl.BlockSpec((rows, width), lambda i: (i, 0))]
    for a in (emb_p, before):
        if a is not None:
            args.append(a)
            in_specs.append(whole(a))
    args += after
    in_specs += [ANY] * len(after)
    if held is not None:
        args.insert(0, held)
        in_specs.insert(0, pl.BlockSpec(memory_space=pltpu.SMEM))
    stats_shape = (8, count) if pack else (count, 256)
    out_shape = [
        jax.ShapeDtypeStruct((count, x.shape[0]), F32),
        jax.ShapeDtypeStruct(stats_shape, F32),
    ]
    out_specs = [
        pl.BlockSpec((count, rows), lambda i: (0, i)),
        pl.BlockSpec(stats_shape, lambda i: (0, 0)),
    ]
    if emb_p is not None:
        out_shape.append(jax.ShapeDtypeStruct((count, count), F32))
        out_specs.append(pl.BlockSpec((count, count), lambda i: (0, 0)))
    return pl.pallas_call(
        kernel,
        grid=(sets,),
        in_specs=in_specs,
        out_specs=out_specs,
        out_shape=out_shape,
        scratch_shapes=[pltpu.VMEM((count, 256), F32)],
        compiler_params=params(),
        cost_estimate=pl.CostEstimate(
            flops=2 * count * x.shape[0] * width,
            bytes_accessed=2 * (count + x.shape[0]) * width,
            transcendentals=2 * count * x.shape[0],
        ),
        name="part_scores",
    )(*args)


def joined(mine, there):
    pad = jnp.zeros((120, mine.shape[1]), F32)
    m = jnp.concatenate([mine, pad], axis=0).T
    t = jnp.concatenate([there, pad], axis=0).T
    top = jnp.maximum(m[:, 0:1], t[:, 0:1])
    return top, m[:, 1:2] * jnp.exp(m[:, 0:1] - top) + t[:, 1:2] * jnp.exp(t[:, 0:1] - top)


def split_rows(x, cols):
    hi = x.astype(BF16).astype(F32)
    mid = (x - hi).astype(BF16).astype(F32)
    low = (x - hi - mid).astype(BF16).astype(F32)
    row = lax.broadcasted_iota(jnp.int32, (TAIL, cols), 0)
    wide = jnp.where(row == 0, hi, jnp.where(row == 1, mid, jnp.where(row == 2, low, 0.0)))
    return wide.astype(BF16)


def joined_rows(x):
    return jnp.sum(x[:, :128].astype(F32), axis=0, keepdims=True)[:, :1]


def guest_rows(mine, there, scores, guests, stays, scale, tile, after):
    count = mine.shape[1]
    n = len(guests)
    part, width = guests[0].shape
    tiles = width // tile

    def kernel(stays_ref, mine_ref, there_ref, *refs):
        s_refs, x_refs = refs[:n], refs[n : 2 * n]
        full, backs, probs = refs[2 * n + 1], refs[2 * n + 2 : -1], refs[-1]

        @pl.when(pl.program_id(0) == 0)
        def _():
            top, total = joined(mine_ref[...], there_ref[...])
            level = scale / total
            for k in range(n):
                probs[:, k * part : (k + 1) * part] = (
                    jnp.exp(s_refs[k][...] - top) * level
                ).astype(BF16)

        far = jnp.zeros((count, tile), F32)
        for k in range(n):
            far += jnp.dot(
                probs[:, k * part : (k + 1) * part], x_refs[k][...], preferred_element_type=F32
            )
        full[...] = far
        far = jnp.where(stays_ref[0] > 0, 0.0, far).astype(BF16)
        for i in range(tiles):

            @pl.when(pl.program_id(0) == i)
            def _():
                backs[i][...] = far

    whole = lambda a: pl.BlockSpec(a.shape, lambda i: (0, 0))
    return pl.pallas_call(
        kernel,
        grid=(tiles,),
        in_specs=[pl.BlockSpec(memory_space=pltpu.SMEM), whole(mine), whole(there)]
        + [whole(s) for s in scores]
        + [pl.BlockSpec((part, tile), lambda i: (0, i))] * n
        + [ANY],
        out_specs=[pl.BlockSpec((count, tile), lambda i: (0, i))]
        + [pl.BlockSpec((count, tile), lambda i: (0, 0))] * tiles,
        out_shape=[jax.ShapeDtypeStruct((count, width), F32)]
        + [jax.ShapeDtypeStruct((count, tile), BF16)] * tiles,
        scratch_shapes=[pltpu.VMEM((count, n * part), BF16)],
        compiler_params=params(),
        cost_estimate=pl.CostEstimate(
            flops=2 * count * n * part * width,
            bytes_accessed=2 * n * part * width + 6 * count * width,
            transcendentals=count * n * part,
        ),
        name="guest_rows",
    )(stays, mine, there, *scores, *guests, after)


def own_grads(mine, there, inner, own, scale):
    count = inner.shape[0]

    def kernel(mine_ref, there_ref, inner_ref, own_ref, out, near, near_t, loss):
        top, total = joined(mine_ref[...], there_ref[...])
        out[...] = (jnp.exp(own_ref[...] - top) * (scale / total)).astype(BF16)
        s = inner_ref[...]
        row = lax.broadcasted_iota(jnp.int32, s.shape, 0)
        col = lax.broadcasted_iota(jnp.int32, s.shape, 1)
        target = jnp.where(row == col, 1.0, 0.0)
        grad = (jnp.exp(s - top) / total - target) * scale
        near[...] = grad.astype(BF16)
        near_t[...] = grad.T.astype(BF16)
        rows = top + jnp.log(total) - jnp.sum(s * target, axis=1, keepdims=True)
        loss[...] = jnp.broadcast_to(jnp.sum(rows, axis=0, keepdims=True), loss.shape)

    wide = jax.ShapeDtypeStruct(own.shape, BF16)
    square = jax.ShapeDtypeStruct((count, count), BF16)
    return pl.pallas_call(
        kernel,
        out_shape=[wide, square, square, jax.ShapeDtypeStruct((8, 128), F32)],
        compiler_params=params(),
        cost_estimate=pl.CostEstimate(
            flops=8 * count * (own.shape[1] + count),
            bytes_accessed=6 * count * (own.shape[1] + count),
            transcendentals=count * (own.shape[1] + count),
        ),
        name="own_grads",
    )(mine, there, inner, own)


def grad_rows(p_own, near, near_t, own, emb_q, emb_p, far, backs, loss, stays, tile, start, before):
    count = near.shape[0]
    tiles = len(backs)
    total, width = own.shape

    def kernel(stays_ref, own_ref, near_ref, near_t_ref, x_ref, q_ref, p_ref, far_ref, *refs):
        back_refs, loss_ref = refs[:tiles], refs[tiles]
        outs, full = refs[-tiles - 1 : -1], refs[-1]
        acc = jnp.dot(near_ref[...], p_ref[...], preferred_element_type=F32)
        acc += jnp.dot(own_ref[...], x_ref[...], preferred_element_type=F32)
        acc += jnp.where(stays_ref[0] > 0, far_ref[...], 0.0)
        full[...] = acc
        pos = jnp.dot(near_t_ref[...], q_ref[...], preferred_element_type=F32).astype(BF16)
        acc = acc.astype(BF16)
        tail = split_rows(loss_ref[0:1, 0:1], tile)
        for i in range(tiles):

            @pl.when(pl.program_id(0) == i)
            def _():
                outs[i][:count] = acc
                outs[i][count : 2 * count] = pos
                outs[i][2 * count : 3 * count] = back_refs[i][...]
                outs[i][3 * count :] = tail

    whole = lambda a: pl.BlockSpec(a.shape, lambda i: (0, 0))
    cut = lambda r: pl.BlockSpec((r, tile), lambda i: (0, start + i))
    args = [stays, p_own, near, near_t, own, emb_q, emb_p, far, *backs, loss, *before]
    return pl.pallas_call(
        kernel,
        grid=(tiles,),
        in_specs=[pl.BlockSpec(memory_space=pltpu.SMEM)]
        + [whole(p_own), whole(near), whole(near_t), cut(total)]
        + [cut(count)] * 3
        + [whole(b) for b in backs]
        + [whole(loss)]
        + [ANY] * len(before),
        out_specs=[pl.BlockSpec((3 * count + TAIL, tile), lambda i: (0, 0))] * tiles
        + [cut(count)],
        out_shape=[jax.ShapeDtypeStruct((3 * count + TAIL, tile), BF16)] * tiles
        + [jax.ShapeDtypeStruct((count, width), F32)],
        input_output_aliases={len(args) - len(before) + i: tiles + i for i in range(len(before))},
        compiler_params=params(),
        cost_estimate=pl.CostEstimate(
            flops=2 * count * (total + 2 * count) * tile * tiles,
            bytes_accessed=(2 * total + 20 * count) * tile * tiles,
            transcendentals=0,
        ),
        name="grad_rows",
    )(*args)


def last_product(pieces, at, count, weight, tile, full=None, after=()):
    kin, width = weight.shape
    n = len(pieces)
    cols = pieces[0].shape[1]

    def kernel(w_ref, *refs):
        out, rows = refs[-2], refs[-1]

        @pl.when(pl.program_id(0) == 0)
        def _():
            for k in range(n):
                piece = refs[k][...]
                if full is not None:
                    piece = refs[n][:, k * cols : (k + 1) * cols] + piece.astype(F32)
                rows[:, k * cols : (k + 1) * cols] = piece.astype(BF16)

        out[...] = dot_t(rows[...], w_ref[...]).astype(BF16)

    args = [weight, *pieces]
    in_specs = [pl.BlockSpec((tile, width), lambda i: (i, 0))]
    in_specs += [pl.BlockSpec((count, cols), lambda i: (at, 0))] * n
    if full is not None:
        args.append(full)
        in_specs.append(pl.BlockSpec((count, width), lambda i: (0, 0)))
    return pl.pallas_call(
        kernel,
        grid=(kin // tile,),
        in_specs=in_specs + [ANY] * len(after),
        out_specs=pl.BlockSpec((count, tile), lambda i: (0, i)),
        out_shape=jax.ShapeDtypeStruct((count, kin), BF16),
        scratch_shapes=[pltpu.VMEM((count, width), BF16)],
        compiler_params=params(),
        cost_estimate=pl.CostEstimate(
            flops=2 * count * width * kin,
            bytes_accessed=2 * width * kin + 4 * count * (width + kin),
            transcendentals=0,
        ),
        name="last_product",
    )(*args, *after)


def weight_part(left, at, rights, base, rows_at, dtype, tails=(), after=()):
    depth, tile = left.shape[1], rights[0].shape[1]
    n, m = len(rights), len(rows_at)
    quarter = left.shape[0] // (8 if at is not None else 4)
    at = at or 0
    first, step = rows_at[0], rows_at[1] - rows_at[0]
    total = m * quarter

    def kernel(left_ref, *refs):
        out = refs[-2] if tails else refs[-1]
        if tails:
            rows = pl.ds(pl.multiple_of(pl.program_id(0) * quarter, quarter), quarter)
        else:
            rows = slice(None)
        for k in range(n):
            cols = slice(k * tile, (k + 1) * tile)
            acc = jnp.dot(left_ref[...], refs[k][...], preferred_element_type=F32)
            if base is not None:
                acc += refs[n][:, cols]
            out[rows, cols] = acc.astype(dtype)
        if tails:
            loss = sum(joined_rows(r[...]) for r in refs[n + 1 : n + 1 + len(tails)])
            out[total:, :] = split_rows(loss, n * tile)
            refs[-1][...] = jnp.broadcast_to(loss, refs[-1].shape)

    in_specs = [pl.BlockSpec((quarter, depth), lambda i: (at + first + step * i, 0))]
    in_specs += [pl.BlockSpec((depth, tile), lambda i: (0, 0))] * n
    args = [left, *rights]
    if base is not None:
        in_specs.append(pl.BlockSpec((quarter, n * tile), lambda i: (first + step * i, 0)))
        args.append(base)
    for t in tails:
        in_specs.append(pl.BlockSpec((TAIL, tile), lambda i: (depth // TAIL, 0)))
        args.append(t)
    in_specs += [ANY] * len(after)
    args += after
    if tails:
        shape = (total + TAIL, n * tile)
        out_shape = [jax.ShapeDtypeStruct(shape, dtype), jax.ShapeDtypeStruct((8, 128), F32)]
        out_specs = [pl.BlockSpec(s.shape, lambda i: (0, 0)) for s in out_shape]
    else:
        out_shape = jax.ShapeDtypeStruct((total, n * tile), dtype)
        out_specs = pl.BlockSpec((quarter, n * tile), lambda i: (i, 0))
    return pl.pallas_call(
        kernel,
        grid=(m,),
        in_specs=in_specs,
        out_specs=out_specs,
        out_shape=out_shape,
        compiler_params=params(),
        cost_estimate=pl.CostEstimate(
            flops=2 * total * n * depth * tile,
            bytes_accessed=2 * depth * (n * tile + total) + 8 * total * n * tile,
            transcendentals=0,
        ),
        name="weight_part",
    )(*args)


def fold_stage(keep, got, loss=None, after=()):
    rows, cols = keep.shape
    mid = rows // 2

    def kernel(keep_ref, got_ref, *refs):
        if loss is None:
            send, rest = refs[-2:]
        else:
            send, rest, state = refs[-3:]
            value = refs[0][0:1, 0:1] + joined_rows(got_ref[rows:])
            state[...] = jnp.broadcast_to(value, state.shape)
            send[mid:] = split_rows(value, cols)
        send[:mid] = (keep_ref[:mid] + got_ref[:mid].astype(F32)).astype(BF16)
        rest[...] = keep_ref[mid:] + got_ref[mid:rows].astype(F32)

    args = [keep, got] + ([loss] if loss is not None else [])
    in_specs = [pl.BlockSpec(memory_space=pltpu.VMEM)] * len(args)
    args += after
    in_specs += [ANY] * len(after)
    out_shape = [
        jax.ShapeDtypeStruct((mid + (TAIL if loss is not None else 0), cols), BF16),
        jax.ShapeDtypeStruct((rows - mid, cols), F32),
    ]
    if loss is not None:
        out_shape.append(jax.ShapeDtypeStruct((8, 128), F32))
    return pl.pallas_call(
        kernel,
        in_specs=in_specs,
        out_shape=out_shape,
        compiler_params=params(),
        cost_estimate=pl.CostEstimate(
            flops=rows * cols, bytes_accessed=9 * rows * cols, transcendentals=0
        ),
        name="fold_stage",
    )(*args)


def last_stage(keeps, gots, loss):
    rows, cols = keeps[0].shape

    def kernel(keep0, got0, keep1, got1, loss_ref, out, state):
        out[:, :cols] = keep0[...] + got0[:rows].astype(F32)
        out[:, cols:] = keep1[...] + got1[:rows].astype(F32)
        state[...] = loss_ref[...] + joined_rows(got0[rows:])

    return pl.pallas_call(
        kernel,
        out_shape=[
            jax.ShapeDtypeStruct((rows, 2 * cols), F32),
            jax.ShapeDtypeStruct((8, 128), F32),
        ],
        compiler_params=params(),
        name="last_stage",
    )(keeps[0], gots[0], keeps[1], gots[1], loss)


def body(queries, passages, weight, bank, neg_ids, block_home):
    count, kin = queries.shape
    width = weight.shape[1]
    scale = 1.0 / (SOFTMAX_TEMPER * math.sqrt(width))
    n_dp = lax.axis_size("dp")
    n_fsdp = lax.axis_size("fsdp")
    devices = n_dp * n_fsdp
    block_rows = bank.shape[1]
    named = neg_ids.shape[1]
    half = n_dp // 2
    me = lax.axis_index("dp")
    core = lax.axis_index("fsdp") % 2
    linear = me * n_fsdp + lax.axis_index("fsdp")

    trip = lambda f: half if f % 2 == 0 else 0

    ids = lax.all_to_all(
        jnp.broadcast_to(neg_ids, (n_dp, named)), "dp", split_axis=0, concat_axis=0, tiled=True
    )
    leaving = jnp.where(ids[0, 0] < 0, jnp.zeros_like(queries), queries)
    visit = move(leaving, trip)
    own, *guests, zero = pick_blocks(bank, ids, block_home, me, n_dp, n_fsdp)
    guests = [
        move(g, lambda f, k=k: k if f % 2 == 0 else k ^ half) for k, g in enumerate(guests)
    ]
    sides = [list(range(half)), list(range(half, n_dp))]
    own = lax.all_to_all(
        own, "dp", split_axis=0, concat_axis=0, tiled=True, axis_index_groups=sides
    )
    late = jnp.where(zero[0, 0] < 0, jnp.zeros_like(passages), passages)

    full_weight = lax.all_gather(weight, "fsdp", axis=0, tiled=True)
    emb_q = jnp.dot(queries, full_weight, preferred_element_type=F32).astype(BF16)
    emb_p = jnp.dot(passages, full_weight, preferred_element_type=F32).astype(BF16)
    emb_v = jnp.dot(visit, full_weight, preferred_element_type=F32).astype(BF16)

    f_bits = [("fsdp", b) for b in bits_of(n_fsdp)]
    d_bits = [("dp", b) for b in bits_of(n_dp)]
    stages = [f_bits[1], d_bits[0]] + f_bits[2:] + d_bits[1:]
    mask = []
    for p in range(devices // 2):
        m = 0
        for s, (axis, bit) in enumerate(stages):
            if not (p >> (len(stages) - 1 - s)) & 1:
                m |= bit if axis == "fsdp" else bit * n_fsdp
        mask.append(m)
    mask = jnp.array(mask, jnp.int32)
    hidden_t = jnp.concatenate([queries, late, visit], axis=0).T
    hidden_t = hidden_t.reshape(devices, kin // devices, -1)
    order = linear ^ jnp.concatenate([mask ^ 1, mask])
    left = jnp.take(hidden_t, order, axis=0).reshape(kin, -1)
    left_in = swap(left[: kin // 2], *f_bits[0])

    masked = n_dp * CAP > named
    own_held, guest_held = None, [None] * half
    if masked:
        owner = block_home[ids] // bank.shape[0] // n_fsdp
        held = lambda g, by: (jnp.sum(owner[g] == by) * block_rows).astype(jnp.int32)
        far = jnp.where(core == 0, 0, half)
        own_held = jnp.stack([held(me, (me & half) + k) for k in range(half)])
        guest_held = [held(me ^ half ^ far, me ^ k ^ far).reshape(1) for k in range(half)]
    rows = CAP * block_rows
    s_own, own_stats, inner = part_scores(
        emb_q, own, rows, own_held, scale, emb_p=emb_p, pack=True
    )
    their_stats = move(own_stats, trip)
    s_guest, stats = [], None
    for k, x in enumerate(guests):
        after = (inner,) if k == half // 2 else ()
        s, stats = part_scores(
            emb_v, x, rows, guest_held[k], scale, before=stats, pack=k == half - 1, after=after
        )
        s_guest.append(s)

    far_stats = move(stats, trip)
    tile = width // 4
    stays = core.astype(jnp.int32).reshape(1)
    far, *backs = guest_rows(
        stats, their_stats, s_guest, guests, stays, scale, tile, left_in
    )
    home = [move(r, trip) for r in backs]
    p_own, near, near_t, loss = own_grads(own_stats, far_stats, inner, s_own, scale)
    rows, kept = [], ()
    for i in range(2):
        *g, full = grad_rows(
            p_own,
            near,
            near_t,
            own,
            emb_q,
            emb_p,
            far,
            backs[2 * i : 2 * i + 2],
            loss,
            stays,
            tile,
            2 * i,
            kept,
        )
        rows += g
        kept = (full,)
    far_rows = [swap(r, *f_bits[0]) for r in rows]

    orders = [stages, [stages[1], stages[0]] + stages[2:]]
    give = ((0, 1), (0, 2))
    hold = ((2, 3), (1, 3))
    every = (0, 1, 2, 3)
    bases = [
        weight_part(left, 4, rows[:2], None, every, F32),
        weight_part(left, 4, rows[2:], None, every, F32, after=(home[0],)),
    ]
    got = [far_rows[:2], far_rows[2:]]
    send, loss = weight_part(
        left_in, None, got[0], bases[0], give[0], BF16, tails=(rows[0], far_rows[0])
    )
    sends = [send, weight_part(left_in, None, got[1], bases[1], give[1], BF16, after=(home[1],))]
    back_p = last_product(rows, 1, count, full_weight, tile, after=(sends[1],))
    keeps = [
        weight_part(left_in, None, got[0], bases[0], hold[0], F32),
        weight_part(left_in, None, got[1], bases[1], hold[1], F32),
    ]
    waits = {(0, 0): (back_p, keeps[1]), (0, 1): (home[2], home[3])}
    for s in range(len(stages)):
        gots = [swap(sends[i], *orders[i][s]) for i in range(2)]
        if s + 1 < len(stages):
            send0, keep0, loss = fold_stage(keeps[0], gots[0], loss, waits.get((s, 0), ()))
            send1, keep1 = fold_stage(keeps[1], gots[1], after=waits.get((s, 1), ()))
            sends, keeps = [send0, send1], [keep0, keep1]
    back_q = last_product(home, 0, count, full_weight, tile, full=full, after=tuple(sends))
    grad_weight, loss = last_stage(keeps, gots, loss)
    loss = loss[0, 0] / (count * devices)
    return (loss, grad_weight, back_q, back_p)


def solution(mesh):
    return jax.shard_map(
        body,
        mesh=mesh,
        in_specs=(
            P(("dp", "fsdp"), None),
            P(("dp", "fsdp"), None),
            P("fsdp", None),
            P(("dp", "fsdp"), None, None),
            P(("dp", "fsdp"), None),
            P(),
        ),
        out_specs=(P(), P(("dp", "fsdp"), None), P(("dp", "fsdp"), None), P(("dp", "fsdp"), None)),
        check_vma=False,
    )
```
